32 devices in a mesh: grp: 2 (over x), comp: 16 (over z, y, core).
Axes of the slice: x: 2, y: 2, z: 4, core: 2. Of those that a mesh axis runs over, the one named last changes fastest.
Arguments:
- spectrum: float32 [1152, 96, 128], P(None, ('grp', 'comp')), parts along dimension 1, may hold values from 0.04 to 14, as said below
- sea_mask: int32 [96, 128], P(('grp', 'comp')), parts along dimension 0, may hold values 0 or 1
- ice_mask: int32 [96, 128], P(('grp', 'comp')), parts along dimension 0, may hold values 0 or 1
- wind: float32 [96, 128], P(('grp', 'comp')), parts along dimension 0, may hold values from 0.2 to 1
- source_matrix: bfloat16 [1152, 1152], replicated, may hold values from -0.1875 to 0.1875
Outputs:
- evolved: float32 [1152, 96, 128], P(None, ('grp', 'comp')), parts along dimension 1
The draws below stay inside these ranges and needn't reach their ends.
There are 2 independent parts, one for each index of `grp`. The reference program is written for one: setup_inputs(seed, part) draws one part's arguments, and reference() takes and returns one part's arrays. A program takes and returns all parts, laid end to end along the dimension named above; an argument that names none is the same for every part. Nothing has to cross between parts.
Inputs may be any that keep to these rules, and one draw needn't show every extreme that they name: `spectrum`: positive spectral densities.
All inputs are finite; a program needn't handle non-finite values. No bound on the sum of `sea_mask` or of `ice_mask` on one device may be relied on, other than what follows from the above.
Results may differ from the reference program's by a relative error of at most 0.0014.
Values sent between devices are 32-bit elements; how exact they have to be, the bound alone decides.
No kernel may reach another device: no remote copies, remote signals or barrier semaphores. Data moves between devices by JAX's collectives and lax.ppermute only.
A program may use at most 64 MiB of HBM per device.

```python
import math
import jax
import jax.numpy as jnp

NDIR = 36
NFREQ = 32
K = 1152
NX = 128
NY = 48
STEPS = 2
SUBSTEPS = 3
SRC_SUB = 3


def draw_spectrum(key, part):
    base_key = jax.random.fold_in(key, 11)
    first_key, second_key, third_key = jax.random.split(base_key, 3)
    baseline = jax.random.uniform(first_key, (K, NY, NX), jnp.float32, 0.5, 1.5)
    cell_scale = jnp.exp(jax.random.uniform(second_key, (1, NY, NX), jnp.float32, math.log(0.3), math.log(3.0)))
    comp_scale = jnp.exp(jax.random.uniform(third_key, (K, 1, 1), jnp.float32, math.log(0.3), math.log(3.0)))
    return baseline * cell_scale * comp_scale


def with_ends(result, stream_key, least, high):
    dims = result.shape
    spot = [jax.random.randint(jax.random.fold_in(stream_key, axis), (), 0, dims[axis]) for axis in range(len(dims))]
    result = result.at[tuple(spot)].set(least)
    longest = dims.index(max(dims))
    spot[longest] = (spot[longest] + 1) % dims[longest]
    return result.at[tuple(spot)].set(high)


def levels(rng, dims, shards, low, high):
    def one(dim, blocks):
        heights = jax.random.uniform(jax.random.fold_in(jax.random.fold_in(rng, 6), dim), (blocks,), jnp.float32, low / len(shards), high / len(shards))
        return jnp.repeat(jnp.exp(heights), dims[dim] // blocks).reshape((-1,) + (1,) * (len(dims) - dim - 1))

    loudness = one(*shards[0])
    for cut in shards[1:]:
        loudness = loudness * one(*cut)
    return loudness


def centred(key, extent, deviation, limit, kind=jnp.bfloat16):
    values = jax.random.normal(key, extent, jnp.float32) * deviation
    return jnp.minimum(jnp.maximum(values, -limit), limit).astype(kind)


def setup_inputs(seed: int = 0, part: int = 0) -> dict:
    arg_keys = jax.random.split(jax.random.key(seed), 6)
    part_splits = jax.random.split(jax.random.fold_in(arg_keys[5], part), 6)
    spectrum = draw_spectrum(jax.random.fold_in(jax.random.fold_in(arg_keys[5], part), 71), part)
    sea_mask = with_ends((jax.random.randint(part_splits[1], (NY, NX), 0, 8) < 7).astype(jnp.int32), jax.random.fold_in(part_splits[1], 1), 0, 1)
    ice_mask = with_ends((jax.random.randint(part_splits[2], (NY, NX), 0, 6) < 1).astype(jnp.int32), jax.random.fold_in(part_splits[2], 1), 0, 1)
    wind = jnp.clip(0.2 + 0.8 * jax.random.uniform(part_splits[3], (NY, NX), jnp.float32) ** levels(part_splits[3], (NY, NX), ((0, 16),), -0.2, 0.2), 0.2, 1.0)
    source_matrix = centred(arg_keys[4], (K, K), K ** -0.5, 0.1875)
    return dict(spectrum=spectrum, sea_mask=sea_mask, ice_mask=ice_mask, wind=wind, source_matrix=source_matrix)


source_rate = 0.5
damping = 0.5


def courant(comp_index):
    direction = (comp_index % NDIR).astype(jnp.float32)
    frequency = (comp_index // NDIR).astype(jnp.float32)
    angles = 2.0 * jnp.pi * (direction + 0.5) / NDIR
    speeds = 0.6 * (0.35 + 0.65 * (NFREQ - 1 - frequency) / (NFREQ - 1))
    return (speeds * jnp.cos(angles))[:, None, None], (speeds * jnp.sin(angles))[:, None, None]


def advance(spectra, courant_x, courant_y):
    western = jnp.roll(spectra, 1, axis=2)
    eastern = jnp.roll(spectra, -1, axis=2)
    zero_row = jnp.zeros_like(spectra[:, :1])
    southern = jnp.concatenate([zero_row, spectra[:, :-1]], axis=1)
    northern = jnp.concatenate([spectra[:, 1:], zero_row], axis=1)
    staying = 1.0 - jnp.abs(courant_x) - jnp.abs(courant_y)
    return (staying * spectra + jnp.maximum(courant_x, 0.0) * western + jnp.maximum(-courant_x, 0.0) * eastern
            + jnp.maximum(courant_y, 0.0) * southern + jnp.maximum(-courant_y, 0.0) * northern)


def sources(spectra, sea, wind, source_matrix):
    layout_shape = spectra.shape
    flattened = spectra.reshape(layout_shape[0], -1)
    sea_flat = sea.reshape(1, -1)
    wind_flat = wind.reshape(1, -1)
    for source_step in range(SRC_SUB):
        rounded = flattened.astype(jnp.bfloat16)
        growth = jnp.dot(source_matrix, rounded, preferred_element_type=jnp.float32)
        energy = jnp.mean(flattened * flattened, axis=0, keepdims=True)
        flattened = sea_flat * (flattened + source_rate * wind_flat * growth) / (1.0 + damping * energy)
    return flattened.reshape(layout_shape)


def reference(spectrum, sea_mask, ice_mask, wind, source_matrix):
    sea = sea_mask.astype(jnp.float32)
    thaw = (1.0 - 0.5 * ice_mask.astype(jnp.float32))[None]
    courant_x, courant_y = courant(jnp.arange(K, dtype=jnp.int32))
    spectra = spectrum
    for outer_step in range(STEPS):
        for inner_step in range(SUBSTEPS):
            spectra = sea[None] * advance(spectra, courant_x, courant_y)
        spectra = sources(spectra, sea, wind, source_matrix) * thaw
    return spectra
```

```python
import functools

import jax
import jax.numpy as jnp
import numpy as np
from jax import lax
from jax.experimental import pallas as pl
from jax.experimental.pallas import tpu as pltpu
from jax.sharding import PartitionSpec as P

NDIR = 36
NFREQ = 32
K = 1152
STEPS = 2
SUBSTEPS = 3
SRC_SUB = 3

source_rate = 0.5
damping = 0.5

SUB = 8
PERIOD = 2 * NDIR
TILES = PERIOD // SUB
BLOCK = 2 * PERIOD
BLOCKS = K // BLOCK
BTILES = 2 * TILES
HALF = BLOCK // 2
HTILES = BTILES // 2


def split_of(positive, tile):
    rows = [positive((tile * SUB + i) % NDIR) for i in range(SUB)]
    if all(rows):
        return 1
    if not any(rows):
        return -1
    return [i for i in range(SUB) if rows[i]]


def north_going(d):
    return d < NDIR // 2


def east_going(d):
    return d < NDIR // 4 or d >= 3 * NDIR // 4


Y_SPLIT = [split_of(north_going, t % TILES) for t in range(BTILES)]
X_SPLIT = [split_of(east_going, t % TILES) for t in range(BTILES)]


def pattern():
    theta = 2.0 * np.pi * ((np.arange(PERIOD) % NDIR) + 0.5) / NDIR
    both = np.stack([np.abs(np.cos(theta)), np.abs(np.sin(theta))])
    return jnp.broadcast_to(jnp.asarray(both, jnp.float32)[:, :, None], (2, PERIOD, 128))


def sublanes(width):
    return lax.broadcasted_iota(jnp.int32, (SUB, width), 0)


def between(rows, iota):
    return (iota >= rows[0]) & (iota <= rows[-1])


def choose(split, iota, yes, no):
    if split == 1:
        return yes
    if split == -1:
        return no
    return jnp.where(between(split, iota), yes, no)


def tile_coefficients(trig_ref, block, t, iota):
    frequency = (block * (BLOCK // NDIR) + (t * SUB) // NDIR).astype(jnp.float32)
    speed = 0.6 * (0.35 + (0.65 / (NFREQ - 1)) * ((NFREQ - 1) - frequency))
    later = 0.6 * 0.65 / (NFREQ - 1)
    first = SUB - ((t * SUB + SUB) % NDIR)
    speeds = jnp.full(iota.shape, speed, jnp.float32)
    if (t * SUB) // NDIR != (t * SUB + SUB - 1) // NDIR:
        speeds = jnp.where(iota >= first, speeds - later, speeds)
    at = pl.ds((t % TILES) * SUB, SUB)
    along = speeds * trig_ref[0, at, :]
    across = speeds * trig_ref[1, at, :]
    return 1.0 - along - across, along, across


def beside(t, iota, value):
    split = X_SPLIT[t]
    west = pltpu.roll(value, 1, 1) if split != -1 else None
    east = pltpu.roll(value, value.shape[1] - 1, 1) if split != 1 else None
    return choose(split, iota, west, east)


def flow(t, iota, rows):
    return [choose(Y_SPLIT[t], iota, rows[i], rows[len(rows) - 1 - i]) for i in range(len(rows))]


def substep(t, iota, coefficients, rows, seas, before):
    staying, along, across = coefficients
    out = []
    for i, row in enumerate(rows):
        upstream = before if i == 0 else rows[i - 1]
        if upstream is None:
            continue
        out.append(seas[i] * (staying * row + along * beside(t, iota, row) + across * upstream))
    return out


def edges(t, iota, coefficients, rows, seas):
    found = [rows[-1]]
    rows, seas = rows[-SUBSTEPS:], seas[-SUBSTEPS:]
    for _ in range(SUBSTEPS - 1):
        rows = substep(t, iota, coefficients, rows, seas, None)
        seas = seas[1:]
        found.append(rows[-1])
    return found


def pack(tiles, iota):
    a, b = tiles[:TILES], tiles[TILES:]
    roll = lambda value, shift: pltpu.roll(value, shift, 0)
    north = [a[0], a[1], a[5], b[0], b[1], b[5],
             jnp.where(iota < 6, a[6], roll(b[2], 6)),
             jnp.where(iota < 6, b[6], roll(a[2], 6)),
             jnp.where(iota < 4, roll(b[4], 4), a[4])]
    south = [a[3], a[7], a[8], b[3], b[7], b[8],
             jnp.where(iota < 2, roll(a[6], 2), a[2]),
             jnp.where(iota < 2, roll(b[6], 2), b[2]),
             jnp.where(iota < 4, a[4], roll(b[4], 4))]
    return north, south


def unpack(north, south, iota):
    roll = lambda value, shift: pltpu.roll(value, shift, 0)
    a = [north[0], north[1], jnp.where(iota < 2, roll(north[7], 2), south[6]), south[0],
         jnp.where(iota < 4, south[8], north[8]), north[2],
         jnp.where(iota < 6, north[6], roll(south[6], 6)), south[1], south[2]]
    b = [north[3], north[4], jnp.where(iota < 2, roll(north[6], 2), south[7]), south[3],
         jnp.where(iota < 4, roll(south[8], 4), roll(north[8], 4)), north[5],
         jnp.where(iota < 6, north[7], roll(south[7], 6)), south[4], south[5]]
    return a + b


def spread(ref, r):
    row = ref[pl.ds(r, 1), :]
    return jnp.broadcast_to(row.astype(jnp.float32), (SUB, row.shape[1]))


def send_edges(block, found, odd, iota, cross_ref, inner_ref):
    for j in range(SUBSTEPS):
        north, south = pack([f[j] for f in found], iota)
        for i in range(HTILES):
            at = pl.ds(block * HALF + i * SUB, SUB)
            cross_ref[j, at, :] = jnp.where(odd, north[i], south[i])
            inner_ref[j, at, :] = jnp.where(odd, south[i], north[i])


def first_kernel(odd_ref, f_ref, sea_ref, trig_ref, cross_ref, inner_ref):
    rows_here = f_ref.shape[0]
    iota = sublanes(f_ref.shape[2])
    odd = odd_ref[0] == 1
    seas = [spread(sea_ref, r) for r in range(rows_here)]

    def block_step(block, carry):
        found = []
        for t in range(BTILES):
            at = pl.ds(block * BLOCK + t * SUB, SUB)
            rows = flow(t, iota, [f_ref[r, at, :] for r in range(rows_here)])
            coefficients = tile_coefficients(trig_ref, block, t, iota)
            found.append(edges(t, iota, coefficients, rows, flow(t, iota, seas)))
        send_edges(block, found, odd, iota, cross_ref, inner_ref)
        return carry

    lax.fori_loop(0, BLOCKS, block_step, 0)


def step_kernel(last, odd_ref, f_ref, sea_ref, ice_ref, wind_ref, trig_ref, matrix_ref, cross_in, inner_in, *rest):
    if last:
        out_ref, f_acc, b_acc = rest
    else:
        out_ref, cross_ref, inner_ref, f_acc, b_acc = rest
    rows_here, comps, width = f_ref.shape
    iota = sublanes(width)
    odd = odd_ref[0] == 1
    seas = [spread(sea_ref, r) for r in range(rows_here)]

    def advance(block, sums):
        halo = []
        for j in range(SUBSTEPS):
            north, south = [], []
            for i in range(HTILES):
                at = pl.ds(block * HALF + i * SUB, SUB)
                cross, inner = cross_in[j, at, :], inner_in[j, at, :]
                north.append(jnp.where(odd, inner, cross))
                south.append(jnp.where(odd, cross, inner))
            halo.append(unpack(north, south, iota))
        done = []
        for t in range(BTILES):
            at = pl.ds(block * BLOCK + t * SUB, SUB)
            rows = flow(t, iota, [f_ref[r, at, :] for r in range(rows_here)])
            flow_seas = flow(t, iota, seas)
            coefficients = tile_coefficients(trig_ref, block, t, iota)
            for j in range(SUBSTEPS):
                rows = substep(t, iota, coefficients, rows, flow_seas, halo[j][t])
            done.append(flow(t, iota, rows))
        sums = list(sums)
        for r in range(rows_here):
            whole = jnp.concatenate([d[r] for d in done], axis=0)
            at = pl.ds(block * BLOCK, BLOCK)
            f_acc[at, r * width:(r + 1) * width] = whole
            b_acc[0, at, r * width:(r + 1) * width] = whole.astype(jnp.bfloat16)
            for d in done:
                sums[r] = sums[r] + d[r] * d[r]
        return tuple(sums)

    zero = jnp.zeros((SUB, width), jnp.float32)
    sums = lax.fori_loop(0, BLOCKS, advance, (zero,) * rows_here)
    energy = jnp.concatenate([jnp.sum(s, axis=0, keepdims=True) for s in sums], axis=1)
    sea = jnp.concatenate([sea_ref[r:r + 1, :].astype(jnp.float32) for r in range(rows_here)], axis=1)
    gain = source_rate * jnp.concatenate([wind_ref[r:r + 1, :] for r in range(rows_here)], axis=1)

    chunk = 384
    for s in range(SRC_SUB):
        scale = sea / (1.0 + (damping / comps) * energy)
        energy = jnp.zeros_like(energy)
        for c in range(comps // chunk):
            at = pl.ds(c * chunk, chunk)
            growth = jnp.dot(matrix_ref[at, :], b_acc[s % 2], preferred_element_type=jnp.float32)
            value = (f_acc[at, :] + gain * growth) * scale
            f_acc[at, :] = value
            if s + 1 < SRC_SUB:
                b_acc[(s + 1) % 2, at, :] = value.astype(jnp.bfloat16)
                energy = energy + jnp.sum(value * value, axis=0, keepdims=True)

    thaw = [1.0 - 0.5 * spread(ice_ref, r) for r in range(rows_here)]

    def finish(block, carry):
        found = []
        for t in range(BTILES):
            at = pl.ds(block * BLOCK + t * SUB, SUB)
            rows = [f_acc[at, r * width:(r + 1) * width] * thaw[r] for r in range(rows_here)]
            for r in range(rows_here):
                out_ref[r, at, :] = rows[r]
            if not last:
                coefficients = tile_coefficients(trig_ref, block, t, iota)
                found.append(edges(t, iota, coefficients, flow(t, iota, rows), flow(t, iota, seas)))
        if not last:
            send_edges(block, found, odd, iota, cross_ref, inner_ref)
        return carry

    lax.fori_loop(0, BLOCKS, finish, 0)


def on_device(spectrum, sea_mask, ice_mask, wind, source_matrix):
    size = lax.axis_size("comp")
    comps, rows_here, width = spectrum.shape
    assert comps == K and rows_here >= SUBSTEPS and size % 2 == 0
    odd = (lax.axis_index("comp") % 2).astype(jnp.int32).reshape(1)
    f = jnp.transpose(spectrum, (1, 0, 2))
    trig = pattern()
    smem = pl.BlockSpec(memory_space=pltpu.SMEM)
    vmem = pl.BlockSpec(memory_space=pltpu.VMEM)
    params = pltpu.CompilerParams(vmem_limit_bytes=32 * 1024 * 1024)
    message = jax.ShapeDtypeStruct((SUBSTEPS, K // 2, width), jnp.float32)
    whole = jax.ShapeDtypeStruct(f.shape, jnp.float32)
    outer_pairs = [(i, i + 1) for i in range(1, size - 1, 2)]
    inner_pairs = [(i, i + 1) for i in range(0, size, 2)]

    def swap(value, pairs):
        return lax.ppermute(value, "comp", pairs + [(j, i) for i, j in pairs])

    cross, inner = pl.pallas_call(
        first_kernel, out_shape=(message, message), in_specs=[smem, vmem, vmem, vmem],
        out_specs=(vmem, vmem), compiler_params=params, name="edges",
    )(odd, f, sea_mask, trig)
    for step in range(STEPS):
        last = step == STEPS - 1
        cross = swap(cross, outer_pairs)
        inner = swap(inner, inner_pairs)
        result = pl.pallas_call(
            functools.partial(step_kernel, last),
            out_shape=(whole,) if last else (whole, message, message),
            in_specs=[smem] + [vmem] * 8,
            out_specs=(vmem,) if last else (vmem,) * 3,
            scratch_shapes=[pltpu.VMEM((K, rows_here * width), jnp.float32),
                            pltpu.VMEM((2, K, rows_here * width), jnp.bfloat16)],
            compiler_params=params, name="outer_step",
        )(odd, f, sea_mask, ice_mask, wind, trig, source_matrix, cross, inner)
        if last:
            f = result[0]
        else:
            f, cross, inner = result
    return jnp.transpose(f, (1, 0, 2))


def solution(mesh):
    return jax.shard_map(
        on_device,
        mesh=mesh,
        in_specs=(
            P(None, ("grp", "comp"), None),
            P(("grp", "comp"), None),
            P(("grp", "comp"), None),
            P(("grp", "comp"), None),
            P(),
        ),
        out_specs=P(None, ("grp", "comp"), None),
        check_vma=False,
    )
```

```python
import functools

import jax
import jax.numpy as jnp
import numpy as np
from jax import lax
from jax.experimental import pallas as pl
from jax.experimental.pallas import tpu as pltpu
from jax.sharding import PartitionSpec as P

NDIR = 36
NFREQ = 32
K = 1152
STEPS = 2
SUBSTEPS = 3
SRC_SUB = 3

source_rate = 0.5
damping = 0.5

SUB = 8
PERIOD = 2 * NDIR
TILES = PERIOD // SUB
BLOCK = 2 * PERIOD
BLOCKS = K // BLOCK
BTILES = 2 * TILES
HALF = BLOCK // 2
HTILES = BTILES // 2


def split_of(positive, tile):
    rows = [positive((tile * SUB + i) % NDIR) for i in range(SUB)]
    if all(rows):
        return 1
    if not any(rows):
        return -1
    return [i for i in range(SUB) if rows[i]]


def north_going(d):
    return d < NDIR // 2


def east_going(d):
    return d < NDIR // 4 or d >= 3 * NDIR // 4


Y_SPLIT = [split_of(north_going, t % TILES) for t in range(BTILES)]
X_SPLIT = [split_of(east_going, t % TILES) for t in range(BTILES)]


def pattern():
    theta = 2.0 * np.pi * ((np.arange(PERIOD) % NDIR) + 0.5) / NDIR
    both = np.stack([np.abs(np.cos(theta)), np.abs(np.sin(theta))]).astype(np.float32)
    return jnp.asarray(np.ascontiguousarray(np.broadcast_to(both[:, :, None], (2, PERIOD, 128))))


def sublanes(width):
    return lax.broadcasted_iota(jnp.int32, (SUB, width), 0)


def between(rows, iota):
    return (iota >= rows[0]) & (iota <= rows[-1])


def choose(split, iota, yes, no):
    if split == 1:
        return yes
    if split == -1:
        return no
    return jnp.where(between(split, iota), yes, no)


def tile_coefficients(trig_ref, block, t, iota):
    frequency = (block * (BLOCK // NDIR) + (t * SUB) // NDIR).astype(jnp.float32)
    speed = 0.6 * (0.35 + (0.65 / (NFREQ - 1)) * ((NFREQ - 1) - frequency))
    later = 0.6 * 0.65 / (NFREQ - 1)
    first = SUB - ((t * SUB + SUB) % NDIR)
    speeds = jnp.full(iota.shape, speed, jnp.float32)
    if (t * SUB) // NDIR != (t * SUB + SUB - 1) // NDIR:
        speeds = jnp.where(iota >= first, speeds - later, speeds)
    at = pl.ds((t % TILES) * SUB, SUB)
    along = speeds * trig_ref[0, at, :]
    across = speeds * trig_ref[1, at, :]
    return 1.0 - along - across, along, across


def beside(t, iota, value):
    split = X_SPLIT[t]
    west = pltpu.roll(value, 1, 1) if split != -1 else None
    east = pltpu.roll(value, value.shape[1] - 1, 1) if split != 1 else None
    return choose(split, iota, west, east)


def flow(t, iota, rows):
    return [choose(Y_SPLIT[t], iota, rows[i], rows[len(rows) - 1 - i]) for i in range(len(rows))]


def substep(t, iota, coefficients, rows, seas, before):
    staying, along, across = coefficients
    out = []
    for i, row in enumerate(rows):
        upstream = before if i == 0 else rows[i - 1]
        if upstream is None:
            continue
        out.append(seas[i] * (staying * row + along * beside(t, iota, row) + across * upstream))
    return out


def edges(t, iota, coefficients, rows, seas, count):
    found = [rows[-1]]
    rows, seas = rows[-count:], seas[-count:]
    for _ in range(count - 1):
        rows = substep(t, iota, coefficients, rows, seas, None)
        seas = seas[1:]
        found.append(rows[-1])
    return found


def pack(tiles, iota):
    a, b = tiles[:TILES], tiles[TILES:]
    roll = lambda value, shift: pltpu.roll(value, shift, 0)
    north = [a[0], a[1], a[5], b[0], b[1], b[5],
             jnp.where(iota < 6, a[6], roll(b[2], 6)),
             jnp.where(iota < 6, b[6], roll(a[2], 6)),
             jnp.where(iota < 4, roll(b[4], 4), a[4])]
    south = [a[3], a[7], a[8], b[3], b[7], b[8],
             jnp.where(iota < 2, roll(a[6], 2), a[2]),
             jnp.where(iota < 2, roll(b[6], 2), b[2]),
             jnp.where(iota < 4, a[4], roll(b[4], 4))]
    return north, south


def unpack(north, south, iota):
    roll = lambda value, shift: pltpu.roll(value, shift, 0)
    a = [north[0], north[1], jnp.where(iota < 2, roll(north[7], 2), south[6]), south[0],
         jnp.where(iota < 4, south[8], north[8]), north[2],
         jnp.where(iota < 6, north[6], roll(south[6], 6)), south[1], south[2]]
    b = [north[3], north[4], jnp.where(iota < 2, roll(north[6], 2), south[7]), south[3],
         jnp.where(iota < 4, roll(south[8], 4), roll(north[8], 4)), north[5],
         jnp.where(iota < 6, north[7], roll(south[7], 6)), south[4], south[5]]
    return a + b


def spread(ref, r):
    row = ref[pl.ds(r, 1), :]
    return jnp.broadcast_to(row.astype(jnp.float32), (SUB, row.shape[1]))


def tile_at(block, t):
    return pl.ds(block * BLOCK + t * SUB, SUB)


def send(block, slot, tiles, odd, iota, cross_ref, inner_ref):
    north, south = pack(tiles, iota)
    for i in range(HTILES):
        at = pl.ds(block * HALF + i * SUB, SUB)
        cross_ref[slot, at, :] = jnp.where(odd, north[i], south[i])
        inner_ref[slot, at, :] = jnp.where(odd, south[i], north[i])


def receive(block, slot, odd, iota, cross_ref, inner_ref):
    north, south = [], []
    for i in range(HTILES):
        at = pl.ds(block * HALF + i * SUB, SUB)
        cross, inner = cross_ref[slot, at, :], inner_ref[slot, at, :]
        north.append(jnp.where(odd, inner, cross))
        south.append(jnp.where(odd, cross, inner))
    return unpack(north, south, iota)


def reader(row_refs):
    if len(row_refs) == 1:
        whole, = row_refs
        return whole.shape, lambda r, at: whole[r, at, :]
    edge, middle = row_refs
    count = middle.shape[0] + 2

    def row(r, at):
        if r == 0:
            return edge[0, at, :]
        if r == count - 1:
            return edge[1, at, :]
        return middle[r - 1, at, :]

    return (count,) + tuple(middle.shape[1:]), row


def edges_kernel(slots, odd_ref, sea_ref, trig_ref, *refs):
    (count, _, width), row = reader(refs[:-2])
    cross_ref, inner_ref = refs[-2:]
    iota = sublanes(width)
    odd = odd_ref[0] == 1
    seas = [spread(sea_ref, r) for r in range(count)]

    def body(block, carry):
        found = []
        for t in range(BTILES):
            rows = flow(t, iota, [row(r, tile_at(block, t)) for r in range(count)])
            coefficients = tile_coefficients(trig_ref, block, t, iota)
            found.append(edges(t, iota, coefficients, rows, flow(t, iota, seas), slots[-1] + 1))
        for i, slot in enumerate(slots):
            send(block, i, [f[slot] for f in found], odd, iota, cross_ref, inner_ref)
        return carry

    lax.fori_loop(0, BLOCKS, body, 0)


def lanes(ref, rows):
    return jnp.concatenate([ref[r:r + 1, :].astype(jnp.float32) for r in rows], axis=1)


def source_steps(rows, sums, sea_ref, wind_ref, matrix_ref, f_acc, b_acc):
    comps = f_acc.shape[0]
    sea, gain = lanes(sea_ref, rows), source_rate * lanes(wind_ref, rows)
    energy = jnp.concatenate([jnp.sum(s, axis=0, keepdims=True) for s in sums], axis=1)
    chunk = comps // 4
    for s in range(SRC_SUB):
        scale = sea / (1.0 + (damping / comps) * energy)
        energy = jnp.zeros_like(energy)
        for c in range(comps // chunk):
            at = pl.ds(c * chunk, chunk)
            growth = jnp.dot(matrix_ref[at, :], b_acc[s % 2], preferred_element_type=jnp.float32)
            value = (f_acc[at, :] + gain * growth) * scale
            f_acc[at, :] = value
            if s + 1 < SRC_SUB:
                b_acc[(s + 1) % 2, at, :] = value.astype(jnp.bfloat16)
                energy = energy + jnp.sum(value * value, axis=0, keepdims=True)


def hold(block, column, tiles, f_acc, b_acc):
    whole = jnp.concatenate(tiles, axis=0)
    width = whole.shape[1]
    at = pl.ds(block * BLOCK, BLOCK)
    f_acc[at, column * width:(column + 1) * width] = whole
    b_acc[0, at, column * width:(column + 1) * width] = whole.astype(jnp.bfloat16)


def middle_kernel(odd_ref, sea_ref, ice_ref, wind_ref, trig_ref, matrix_ref, cross_ref, inner_ref, *refs):
    (count, _, width), row = reader(refs[:-4])
    middle_ref, edge_ref, f_acc, b_acc = refs[-4:]
    iota = sublanes(width)
    odd = odd_ref[0] == 1
    seas = [spread(sea_ref, r) for r in range(count)]
    between_rows = range(1, count - 1)

    def advance(block, sums):
        halo = [receive(block, j, odd, iota, cross_ref, inner_ref) for j in range(SUBSTEPS - 1)]
        done = []
        for t in range(BTILES):
            rows = flow(t, iota, [row(r, tile_at(block, t)) for r in range(count)])
            flow_seas = flow(t, iota, seas)
            coefficients = tile_coefficients(trig_ref, block, t, iota)
            for j in range(SUBSTEPS):
                before = halo[j][t] if j < SUBSTEPS - 1 else jnp.zeros_like(rows[0])
                rows = substep(t, iota, coefficients, rows, flow_seas, before)
            rows = flow(t, iota, rows)
            edge_ref[0, tile_at(block, t), :] = rows[0]
            edge_ref[1, tile_at(block, t), :] = rows[-1]
            done.append(rows)
        sums = list(sums)
        for i, r in enumerate(between_rows):
            hold(block, i, [d[r] for d in done], f_acc, b_acc)
            for d in done:
                sums[i] = sums[i] + d[r] * d[r]
        return tuple(sums)

    zero = jnp.zeros((SUB, width), jnp.float32)
    sums = lax.fori_loop(0, BLOCKS, advance, (zero,) * len(between_rows))
    source_steps(between_rows, sums, sea_ref, wind_ref, matrix_ref, f_acc, b_acc)
    for i, r in enumerate(between_rows):
        middle_ref[i] = f_acc[:, i * width:(i + 1) * width] * (1.0 - 0.5 * ice_ref[r:r + 1, :].astype(jnp.float32))


def edge_kernel(last, odd_ref, sea_ref, ice_ref, wind_ref, trig_ref, matrix_ref, cross_in, inner_in, part_ref, middle_ref, *refs):
    f_acc, b_acc = refs[-2:]
    out_ref = refs[0]
    count, width = middle_ref.shape[0] + 2, middle_ref.shape[2]
    iota = sublanes(width)
    odd = odd_ref[0] == 1
    seas = [spread(sea_ref, r) for r in range(count)]
    edge_rows = (0, count - 1)

    def advance(block, sums):
        halo = receive(block, 0, odd, iota, cross_in, inner_in)
        first, final = [], []
        for t in range(BTILES):
            _, _, across = tile_coefficients(trig_ref, block, t, iota)
            term = flow(t, iota, seas)[0] * (across * halo[t])
            zero = jnp.zeros_like(term)
            at = tile_at(block, t)
            first.append(part_ref[0, at, :] + choose(Y_SPLIT[t], iota, term, zero))
            final.append(part_ref[1, at, :] + choose(Y_SPLIT[t], iota, zero, term))
        sums = list(sums)
        for i, tiles in enumerate((first, final)):
            hold(block, i, tiles, f_acc, b_acc)
            for tile in tiles:
                sums[i] = sums[i] + tile * tile
        return tuple(sums)

    zero = jnp.zeros((SUB, width), jnp.float32)
    sums = lax.fori_loop(0, BLOCKS, advance, (zero, zero))
    source_steps(edge_rows, sums, sea_ref, wind_ref, matrix_ref, f_acc, b_acc)
    thaw = [1.0 - 0.5 * spread(ice_ref, r) for r in edge_rows]
    if last:
        for i, r in enumerate(edge_rows):
            out_ref[r] = f_acc[:, i * width:(i + 1) * width] * thaw[i][:1]
        for r in range(1, count - 1):
            out_ref[r] = middle_ref[r - 1]
        return
    cross_ref, inner_ref = refs[1:3]

    def finish(block, carry):
        found = []
        for t in range(BTILES):
            at = tile_at(block, t)
            ends = [f_acc[at, i * width:(i + 1) * width] * thaw[i] for i in range(2)]
            out_ref[0, at, :], out_ref[1, at, :] = ends
            rows = flow(t, iota, [ends[0]] + [middle_ref[r - 1, at, :] for r in range(1, count - 1)] + [ends[1]])
            coefficients = tile_coefficients(trig_ref, block, t, iota)
            found.append(edges(t, iota, coefficients, rows, flow(t, iota, seas), SUBSTEPS - 1))
        for slot in range(SUBSTEPS - 1):
            send(block, slot, [f[slot] for f in found], odd, iota, cross_ref, inner_ref)
        return carry

    lax.fori_loop(0, BLOCKS, finish, 0)


def on_device(spectrum, sea_mask, ice_mask, wind, source_matrix):
    size = lax.axis_size("comp")
    comps, count, width = spectrum.shape
    assert comps == K and count >= SUBSTEPS and size % 2 == 0
    odd = (lax.axis_index("comp") % 2).astype(jnp.int32).reshape(1)
    f = jnp.transpose(spectrum, (1, 0, 2))
    trig = pattern()
    outer_pairs = [(i, i + 1) for i in range(1, size - 1, 2)]
    inner_pairs = [(i, i + 1) for i in range(0, size, 2)]

    def swap(messages):
        cross, inner = messages
        return tuple(lax.ppermute(value, "comp", pairs + [(j, i) for i, j in pairs])
                     for value, pairs in ((cross, outer_pairs), (inner, inner_pairs)))

    def call(kernel, name, args, outs, scratch_rows=0):
        scratch = []
        if scratch_rows:
            scratch = [pltpu.VMEM((K, scratch_rows * width), jnp.float32),
                       pltpu.VMEM((2, K, scratch_rows * width), jnp.bfloat16)]
        vmem = pl.BlockSpec(memory_space=pltpu.VMEM)
        return pl.pallas_call(
            kernel, out_shape=[jax.ShapeDtypeStruct(s, jnp.float32) for s in outs],
            in_specs=[pl.BlockSpec(memory_space=pltpu.SMEM)] + [vmem] * len(args),
            out_specs=[vmem] * len(outs), scratch_shapes=scratch, name=name,
            compiler_params=pltpu.CompilerParams(vmem_limit_bytes=24 * 1024 * 1024),
        )(odd, *args)

    def message(slots):
        return [(slots, K // 2, width)] * 2

    early, late = tuple(range(SUBSTEPS - 1)), (SUBSTEPS - 1,)
    rows = (f,)
    masks = (sea_mask, ice_mask, wind, trig, source_matrix)
    sent = call(functools.partial(edges_kernel, early), "early_edges", (sea_mask, trig) + rows, message(SUBSTEPS - 1))
    for step in range(STEPS):
        came = swap(sent)
        sent = call(functools.partial(edges_kernel, late), "late_edges", (sea_mask, trig) + rows, message(1))
        came_late = swap(sent)
        middle, part = call(middle_kernel, "middle_rows", masks + came + rows,
                            [(count - 2, K, width), (2, K, width)], count - 2)
        last = step == STEPS - 1
        outs = [(count, K, width)] if last else [(2, K, width)] + message(SUBSTEPS - 1)
        result = call(functools.partial(edge_kernel, last), "edge_rows", masks + came_late + (part, middle), outs, 2)
        if last:
            return jnp.transpose(result[0], (1, 0, 2))
        rows, sent = (result[0], middle), result[1:]


def solution(mesh):
    return jax.shard_map(
        on_device,
        mesh=mesh,
        in_specs=(
            P(None, ("grp", "comp"), None),
            P(("grp", "comp"), None),
            P(("grp", "comp"), None),
            P(("grp", "comp"), None),
            P(),
        ),
        out_specs=P(None, ("grp", "comp"), None),
        check_vma=False,
    )
```

```python
import functools

import jax
import jax.numpy as jnp
import numpy as np
from jax import lax
from jax.experimental import pallas as pl
from jax.experimental.pallas import tpu as pltpu
from jax.sharding import PartitionSpec as P

NDIR = 36
NFREQ = 32
K = 1152
STEPS = 2
SUBSTEPS = 3
SRC_SUB = 3

source_rate = 0.5
damping = 0.5

SUB = 8
PERIOD = 2 * NDIR
TILES = PERIOD // SUB
BLOCK = 2 * PERIOD
BLOCKS = K // BLOCK
BTILES = 2 * TILES
HALF = BLOCK // 2
HTILES = BTILES // 2
CHUNKS = 4


def split_of(positive, tile):
    rows = [positive((tile * SUB + i) % NDIR) for i in range(SUB)]
    if all(rows):
        return 1
    if not any(rows):
        return -1
    return [i for i in range(SUB) if rows[i]]


def north_going(d):
    return d < NDIR // 2


def east_going(d):
    return d < NDIR // 4 or d >= 3 * NDIR // 4


Y_SPLIT = [split_of(north_going, t % TILES) for t in range(BTILES)]
X_SPLIT = [split_of(east_going, t % TILES) for t in range(BTILES)]


def pattern():
    theta = 2.0 * np.pi * ((np.arange(PERIOD) % NDIR) + 0.5) / NDIR
    both = np.stack([np.abs(np.cos(theta)), np.abs(np.sin(theta))]).astype(np.float32)
    return jnp.asarray(np.ascontiguousarray(np.broadcast_to(both[:, :, None], (2, PERIOD, 128))))


def sublanes(width):
    return lax.broadcasted_iota(jnp.int32, (SUB, width), 0)


def between(rows, iota):
    return (iota >= rows[0]) & (iota <= rows[-1])


def choose(split, iota, yes, no):
    if split == 1:
        return yes
    if split == -1:
        return no
    return jnp.where(between(split, iota), yes, no)


def tile_coefficients(trig_ref, block, t, iota):
    frequency = (block * (BLOCK // NDIR) + (t * SUB) // NDIR).astype(jnp.float32)
    speed = 0.6 * (0.35 + (0.65 / (NFREQ - 1)) * ((NFREQ - 1) - frequency))
    later = 0.6 * 0.65 / (NFREQ - 1)
    first = SUB - ((t * SUB + SUB) % NDIR)
    speeds = jnp.full(iota.shape, speed, jnp.float32)
    if (t * SUB) // NDIR != (t * SUB + SUB - 1) // NDIR:
        speeds = jnp.where(iota >= first, speeds - later, speeds)
    at = pl.ds((t % TILES) * SUB, SUB)
    along = speeds * trig_ref[0, at, :]
    across = speeds * trig_ref[1, at, :]
    return 1.0 - along - across, along, across


def beside(t, iota, value):
    split = X_SPLIT[t]
    west = pltpu.roll(value, 1, 1) if split != -1 else None
    east = pltpu.roll(value, value.shape[1] - 1, 1) if split != 1 else None
    return choose(split, iota, west, east)


def flow(t, iota, rows):
    return [choose(Y_SPLIT[t], iota, rows[i], rows[len(rows) - 1 - i]) for i in range(len(rows))]


def substep(t, iota, coefficients, rows, seas, before):
    staying, along, across = coefficients
    out = []
    for i, row in enumerate(rows):
        upstream = before if i == 0 else rows[i - 1]
        if upstream is None:
            continue
        out.append(seas[i] * (staying * row + along * beside(t, iota, row) + across * upstream))
    return out


def edges(t, iota, coefficients, rows, seas, count):
    found = [rows[-1]]
    rows, seas = rows[-count:], seas[-count:]
    for _ in range(count - 1):
        rows = substep(t, iota, coefficients, rows, seas, None)
        seas = seas[1:]
        found.append(rows[-1])
    return found


def pack(tiles, iota):
    a, b = tiles[:TILES], tiles[TILES:]
    roll = lambda value, shift: pltpu.roll(value, shift, 0)
    north = [a[0], a[1], a[5], b[0], b[1], b[5],
             jnp.where(iota < 6, a[6], roll(b[2], 6)),
             jnp.where(iota < 6, b[6], roll(a[2], 6)),
             jnp.where(iota < 4, roll(b[4], 4), a[4])]
    south = [a[3], a[7], a[8], b[3], b[7], b[8],
             jnp.where(iota < 2, roll(a[6], 2), a[2]),
             jnp.where(iota < 2, roll(b[6], 2), b[2]),
             jnp.where(iota < 4, a[4], roll(b[4], 4))]
    return north, south


def unpack(north, south, iota):
    roll = lambda value, shift: pltpu.roll(value, shift, 0)
    a = [north[0], north[1], jnp.where(iota < 2, roll(north[7], 2), south[6]), south[0],
         jnp.where(iota < 4, south[8], north[8]), north[2],
         jnp.where(iota < 6, north[6], roll(south[6], 6)), south[1], south[2]]
    b = [north[3], north[4], jnp.where(iota < 2, roll(north[6], 2), south[7]), south[3],
         jnp.where(iota < 4, roll(south[8], 4), roll(north[8], 4)), north[5],
         jnp.where(iota < 6, north[7], roll(south[7], 6)), south[4], south[5]]
    return a + b


def spread(ref, r):
    row = ref[pl.ds(r, 1), :]
    return jnp.broadcast_to(row.astype(jnp.float32), (SUB, row.shape[1]))


def tile_at(block, t):
    return pl.ds(block * BLOCK + t * SUB, SUB)


def send(block, slot, tiles, odd, iota, cross_ref, inner_ref):
    north, south = pack(tiles, iota)
    for i in range(HTILES):
        at = pl.ds(block * HALF + i * SUB, SUB)
        cross_ref[slot, at, :] = jnp.where(odd, north[i], south[i])
        inner_ref[slot, at, :] = jnp.where(odd, south[i], north[i])


def receive(block, slot, odd, iota, cross_ref, inner_ref):
    north, south = [], []
    for i in range(HTILES):
        at = pl.ds(block * HALF + i * SUB, SUB)
        cross, inner = cross_ref[slot, at, :], inner_ref[slot, at, :]
        north.append(jnp.where(odd, inner, cross))
        south.append(jnp.where(odd, cross, inner))
    return unpack(north, south, iota)


def reader(row_refs):
    if len(row_refs) == 1:
        whole, = row_refs
        return whole.shape, lambda r, at: whole[r, at, :]
    edge, middle = row_refs
    count = middle.shape[0] + 2

    def row(r, at):
        if r == 0:
            return edge[0, at, :]
        if r == count - 1:
            return edge[1, at, :]
        return middle[r - 1, at, :]

    return (count,) + tuple(middle.shape[1:]), row


def edges_body(slots, block, row, count, seas, trig_ref, odd, iota, cross_ref, inner_ref):
    found = []
    for t in range(BTILES):
        rows = flow(t, iota, [row(r, tile_at(block, t)) for r in range(count)])
        coefficients = tile_coefficients(trig_ref, block, t, iota)
        found.append(edges(t, iota, coefficients, rows, flow(t, iota, seas), slots[-1] + 1))
    for i, slot in enumerate(slots):
        send(block, i, [f[slot] for f in found], odd, iota, cross_ref, inner_ref)


def first_kernel(slots, odd_ref, f_hbm, sea_hbm, trig_hbm, f_ref, sea_ref, trig_ref, cross_ref, inner_ref, sem, block_sem):
    count, _, width = f_ref.shape

    def block_copy(block):
        at = pl.ds(pl.multiple_of(block * BLOCK, BLOCK), BLOCK)
        return pltpu.make_async_copy(f_hbm.at[:, at, :], f_ref.at[:, at, :], block_sem.at[block])

    small = [pltpu.make_async_copy(sea_hbm, sea_ref, sem.at[0]), pltpu.make_async_copy(trig_hbm, trig_ref, sem.at[1])]
    for copy in small:
        copy.start()
    for block in range(BLOCKS):
        block_copy(block).start()
    for copy in small:
        copy.wait()
    iota = sublanes(width)
    odd = odd_ref[0] == 1
    seas = [spread(sea_ref, r) for r in range(count)]

    def body(block, carry):
        block_copy(block).wait()
        edges_body(slots, block, lambda r, at: f_ref[r, at, :], count, seas, trig_ref, odd, iota, cross_ref, inner_ref)
        return carry

    lax.fori_loop(0, BLOCKS, body, 0)


def edges_kernel(slots, odd_ref, sea_ref, trig_ref, *refs):
    (count, _, width), row = reader(refs[:-2])
    cross_ref, inner_ref = refs[-2:]
    iota = sublanes(width)
    odd = odd_ref[0] == 1
    seas = [spread(sea_ref, r) for r in range(count)]

    def body(block, carry):
        edges_body(slots, block, row, count, seas, trig_ref, odd, iota, cross_ref, inner_ref)
        return carry

    lax.fori_loop(0, BLOCKS, body, 0)


def local_kernel(sea_ref, trig_ref, *refs):
    (count, _, width), row = reader(refs[:-1])
    local_ref = refs[-1]
    iota = sublanes(width)
    seas = [spread(sea_ref, r) for r in range(count)]

    def body(block, carry):
        for t in range(BTILES):
            at = tile_at(block, t)
            rows = flow(t, iota, [row(r, at) for r in range(count)])
            coefficients = tile_coefficients(trig_ref, block, t, iota)
            for _ in range(SUBSTEPS):
                rows = substep(t, iota, coefficients, rows, flow(t, iota, seas), jnp.zeros_like(rows[0]))
            for r, value in enumerate(flow(t, iota, rows)):
                local_ref[r, at, :] = value
        return carry

    lax.fori_loop(0, BLOCKS, body, 0)


def upstream_part(t, iota, coefficients, seas, halo):
    staying, along, across = coefficients
    rows = []
    for j in range(SUBSTEPS):
        new = []
        for i in range(j + 1):
            value = None
            if i < len(rows):
                value = staying * rows[i] + along * beside(t, iota, rows[i])
            upstream = rows[i - 1] if i else (halo[j] if j < len(halo) else None)
            if upstream is not None:
                value = across * upstream if value is None else value + across * upstream
            new.append(seas[i] * value)
        rows = new
    return rows


def lanes(ref, rows):
    return jnp.concatenate([ref[r:r + 1, :].astype(jnp.float32) for r in rows], axis=1)


def source_steps(rows, sums, sea_ref, ice_ref, wind_ref, matrix_ref, f_acc, b_acc, ready=None):
    comps = f_acc.shape[0]
    sea, gain = lanes(sea_ref, rows), source_rate * lanes(wind_ref, rows)
    energy = jnp.concatenate([jnp.sum(s, axis=0, keepdims=True) for s in sums], axis=1)
    chunk = comps // CHUNKS
    for s in range(SRC_SUB):
        scale = sea / (1.0 + (damping / comps) * energy)
        energy = jnp.zeros_like(energy)
        if s + 1 == SRC_SUB:
            scale = scale * (1.0 - 0.5 * lanes(ice_ref, rows))
        for c in range(comps // chunk):
            at = pl.ds(c * chunk, chunk)
            growth = jnp.dot(matrix_ref[at, :], b_acc[s % 2], preferred_element_type=jnp.float32)
            value = (f_acc[at, :] + gain * growth) * scale
            f_acc[at, :] = value
            if s + 1 < SRC_SUB:
                b_acc[(s + 1) % 2, at, :] = value.astype(jnp.bfloat16)
                energy = energy + jnp.sum(value * value, axis=0, keepdims=True)
            elif ready is not None:
                ready(c, at)


def hold(block, column, tiles, f_acc, b_acc):
    whole = jnp.concatenate(tiles, axis=0)
    width = whole.shape[1]
    at = pl.ds(block * BLOCK, BLOCK)
    f_acc[at, column * width:(column + 1) * width] = whole
    b_acc[0, at, column * width:(column + 1) * width] = whole.astype(jnp.bfloat16)


def middle_kernel(odd_ref, sea_ref, ice_ref, wind_ref, trig_ref, matrix_ref, cross_ref, inner_ref, local_ref,
                  middle_ref, edge_ref, f_acc, b_acc):
    count, _, width = local_ref.shape
    iota = sublanes(width)
    odd = odd_ref[0] == 1
    seas = [spread(sea_ref, r) for r in range(count)]
    between_rows = range(1, count - 1)

    def advance(block, sums):
        halo = [receive(block, j, odd, iota, cross_ref, inner_ref) for j in range(SUBSTEPS - 1)]
        done = []
        for t in range(BTILES):
            at = tile_at(block, t)
            coefficients = tile_coefficients(trig_ref, block, t, iota)
            rows = upstream_part(t, iota, coefficients, flow(t, iota, seas), [h[t] for h in halo])
            rows = flow(t, iota, rows + [jnp.zeros_like(rows[0])] * (count - len(rows)))
            rows = [local_ref[r, at, :] + value for r, value in enumerate(rows)]
            edge_ref[0, at, :] = rows[0]
            edge_ref[1, at, :] = rows[-1]
            done.append(rows)
        sums = list(sums)
        for i, r in enumerate(between_rows):
            hold(block, i, [d[r] for d in done], f_acc, b_acc)
            for d in done:
                sums[i] = sums[i] + d[r] * d[r]
        return tuple(sums)

    zero = jnp.zeros((SUB, width), jnp.float32)
    sums = lax.fori_loop(0, BLOCKS, advance, (zero,) * len(between_rows))
    source_steps(between_rows, sums, sea_ref, ice_ref, wind_ref, matrix_ref, f_acc, b_acc)
    for i in range(count - 2):
        middle_ref[i] = f_acc[:, i * width:(i + 1) * width]


def edge_kernel(last, odd_ref, sea_ref, ice_ref, wind_ref, trig_ref, matrix_ref, cross_in, inner_in, part_ref, middle_ref, *refs):
    if last:
        out_ref, f_acc, b_acc, sem = refs
    else:
        out_ref, cross_ref, inner_ref, f_acc, b_acc = refs
    count, width = middle_ref.shape[0] + 2, middle_ref.shape[2]
    iota = sublanes(width)
    odd = odd_ref[0] == 1
    seas = [spread(sea_ref, r) for r in range(count)]
    edge_rows = (0, count - 1)

    def advance(block, sums):
        halo = receive(block, 0, odd, iota, cross_in, inner_in)
        first, final = [], []
        for t in range(BTILES):
            _, _, across = tile_coefficients(trig_ref, block, t, iota)
            term = flow(t, iota, seas)[0] * (across * halo[t])
            zero = jnp.zeros_like(term)
            at = tile_at(block, t)
            first.append(part_ref[0, at, :] + choose(Y_SPLIT[t], iota, term, zero))
            final.append(part_ref[1, at, :] + choose(Y_SPLIT[t], iota, zero, term))
        sums = list(sums)
        for i, tiles in enumerate((first, final)):
            hold(block, i, tiles, f_acc, b_acc)
            for tile in tiles:
                sums[i] = sums[i] + tile * tile
        return tuple(sums)

    zero = jnp.zeros((SUB, width), jnp.float32)
    sums = lax.fori_loop(0, BLOCKS, advance, (zero, zero))
    if last:
        copies = [pltpu.make_async_copy(middle_ref, out_ref.at[pl.ds(1, count - 2)], sem.at[2 * CHUNKS])]
        copies[0].start()

        def ready(c, at):
            for i, r in enumerate(edge_rows):
                columns = pl.ds(i * width, width)
                copy = pltpu.make_async_copy(f_acc.at[at, columns], out_ref.at[r, at, :], sem.at[2 * c + i])
                copy.start()
                copies.append(copy)

        source_steps(edge_rows, sums, sea_ref, ice_ref, wind_ref, matrix_ref, f_acc, b_acc, ready)
        for copy in copies:
            copy.wait()
        return
    source_steps(edge_rows, sums, sea_ref, ice_ref, wind_ref, matrix_ref, f_acc, b_acc)

    def finish(block, carry):
        found = []
        for t in range(BTILES):
            at = tile_at(block, t)
            ends = [f_acc[at, i * width:(i + 1) * width] for i in range(2)]
            out_ref[0, at, :], out_ref[1, at, :] = ends
            rows = flow(t, iota, [ends[0]] + [middle_ref[r - 1, at, :] for r in range(1, count - 1)] + [ends[1]])
            coefficients = tile_coefficients(trig_ref, block, t, iota)
            found.append(edges(t, iota, coefficients, rows, flow(t, iota, seas), SUBSTEPS - 1))
        for slot in range(SUBSTEPS - 1):
            send(block, slot, [f[slot] for f in found], odd, iota, cross_ref, inner_ref)
        return carry

    lax.fori_loop(0, BLOCKS, finish, 0)


def on_device(spectrum, sea_mask, ice_mask, wind, source_matrix):
    size = lax.axis_size("comp")
    comps, count, width = spectrum.shape
    assert comps == K and count >= SUBSTEPS and size % 2 == 0
    odd = (lax.axis_index("comp") % 2).astype(jnp.int32).reshape(1)
    f = jnp.transpose(spectrum, (1, 0, 2))
    trig = pattern()
    outer_pairs = [(i, i + 1) for i in range(1, size - 1, 2)]
    inner_pairs = [(i, i + 1) for i in range(0, size, 2)]

    def swap(messages):
        cross, inner = messages
        return tuple(lax.ppermute(value, "comp", pairs + [(j, i) for i, j in pairs])
                     for value, pairs in ((cross, outer_pairs), (inner, inner_pairs)))

    vmem = pl.BlockSpec(memory_space=pltpu.VMEM)
    hbm = pl.BlockSpec(memory_space=pltpu.HBM)
    dma = pltpu.SemaphoreType.DMA

    def call(kernel, name, args, outs, scratch_rows=0, scratch=(), in_space=vmem, out_space=vmem, scalar=True, limit=24):
        scratch = list(scratch)
        if scratch_rows:
            scratch = [pltpu.VMEM((K, scratch_rows * width), jnp.float32),
                       pltpu.VMEM((2, K, scratch_rows * width), jnp.bfloat16)] + scratch
        outs = [out if hasattr(out, "dtype") else jax.ShapeDtypeStruct(out, jnp.float32) for out in outs]
        return pl.pallas_call(
            kernel, out_shape=outs, name=name,
            in_specs=[pl.BlockSpec(memory_space=pltpu.SMEM)] * scalar + [in_space] * len(args),
            out_specs=[out_space] * len(outs), scratch_shapes=scratch,
            compiler_params=pltpu.CompilerParams(vmem_limit_bytes=limit * 1024 * 1024),
        )(*((odd,) if scalar else ()), *args)

    def message(slots):
        return [(slots, K // 2, width)] * 2

    early, late = tuple(range(SUBSTEPS - 1)), (SUBSTEPS - 1,)
    f, sea, trig, *sent = call(
        functools.partial(first_kernel, early), "first_edges", [pltpu.with_memory_space_constraint(x, pltpu.HBM) for x in (f, sea_mask, trig)],
        [f, sea_mask, trig] + message(SUBSTEPS - 1), scratch=[dma((2,)), dma((BLOCKS,))], in_space=hbm, limit=24)
    rows = (f,)
    masks = (sea, ice_mask, wind, trig, source_matrix)
    for step in range(STEPS):
        came = swap(sent)
        sent = call(functools.partial(edges_kernel, late), "late_edges", (sea, trig) + rows, message(1))
        came_late = swap(sent)
        local, = call(local_kernel, "local_rows", (sea, trig) + rows, [(count, K, width)], scalar=False)
        middle, part = call(middle_kernel, "middle_rows", masks + came + (local,),
                            [(count - 2, K, width), (2, K, width)], count - 2)
        last = step == STEPS - 1
        outs = [(count, K, width)] if last else [(2, K, width)] + message(SUBSTEPS - 1)
        result = call(functools.partial(edge_kernel, last), "edge_rows", masks + came_late + (part, middle), outs, 2,
                      scratch=[dma((2 * CHUNKS + 1,))] if last else (), out_space=hbm if last else vmem)
        if last:
            return jnp.transpose(result[0], (1, 0, 2))
        rows, sent = (result[0], middle), result[1:]


def solution(mesh):
    return jax.shard_map(
        on_device,
        mesh=mesh,
        in_specs=(
            P(None, ("grp", "comp"), None),
            P(("grp", "comp"), None),
            P(("grp", "comp"), None),
            P(("grp", "comp"), None),
            P(),
        ),
        out_specs=P(None, ("grp", "comp"), None),
        check_vma=False,
    )
```

```python
import functools

import jax
import jax.numpy as jnp
import numpy as np
from jax import lax
from jax.experimental import pallas as pl
from jax.experimental.pallas import tpu as pltpu
from jax.sharding import PartitionSpec as P

NDIR = 36
NFREQ = 32
K = 1152
STEPS = 2
SUBSTEPS = 3
SRC_SUB = 3

source_rate = 0.5
damping = 0.5

SUB = 8
QUADRANTS = 4
ARC = NDIR // QUADRANTS
ARC_ROWS = SUB * ARC
BLOCK = QUADRANTS * ARC_ROWS
BLOCKS = K // BLOCK
HALF = BLOCK // 2
CHUNKS = 4
EAST = (True, False, False, True)
NORTH = (True, True, False, False)


def source_row(row):
    quadrant, rest = divmod(row, ARC_ROWS)
    frequency, direction = divmod(rest, ARC)
    return frequency * NDIR + quadrant * ARC + direction


ORDER = [source_row(row) for row in range(BLOCK)]
INVERSE = [ORDER.index(row) for row in range(BLOCK)]


def reorder(read, order, tile, iota):
    pieces = {}
    for to, row in enumerate(order[tile * SUB:(tile + 1) * SUB]):
        pieces.setdefault((row // SUB, (to - row) % SUB), []).append(to)
    out = None
    for (index, shift), rows in pieces.items():
        value = read(index)
        if shift:
            value = pltpu.roll(value, shift, 0)
        out = value if out is None else jnp.where((iota >= rows[0]) & (iota <= rows[-1]), value, out)
    return out


def pattern():
    row = np.arange(ARC_ROWS)
    theta = 2.0 * np.pi * (row % ARC + 0.5) / NDIR
    slower = 0.6 * 0.65 / (NFREQ - 1) * (row // ARC)
    table = np.stack([np.cos(theta), np.sin(theta), slower]).astype(np.float32)
    return jnp.asarray(np.ascontiguousarray(np.broadcast_to(table[:, :, None], (3, ARC_ROWS, 128))))


def sublanes(width):
    return lax.broadcasted_iota(jnp.int32, (SUB, width), 0)


def arc_coefficients(trig_ref, block, i):
    frequency = (block * SUB).astype(jnp.float32)
    fastest = 0.6 * (0.35 + (0.65 / (NFREQ - 1)) * ((NFREQ - 1) - frequency))
    at = pl.ds(i * SUB, SUB)
    speed = fastest - trig_ref[2, at, :]
    one, other = speed * trig_ref[0, at, :], speed * trig_ref[1, at, :]
    return 1.0 - one - other, one, other


def tiles(trig_ref, block):
    for i in range(ARC):
        staying, one, other = arc_coefficients(trig_ref, block, i)
        for q in range(QUADRANTS):
            at = pl.ds(block * BLOCK + q * ARC_ROWS + i * SUB, SUB)
            yield q, i, at, (staying, one, other) if q % 2 == 0 else (staying, other, one)


def beside(q, value):
    return pltpu.roll(value, 1 if EAST[q] else value.shape[1] - 1, 1)


def flow(q, rows):
    return list(rows) if NORTH[q] else list(rows)[::-1]


def substep(q, coefficients, rows, seas, whole):
    staying, along, across = coefficients
    out = []
    for i, row in enumerate(rows):
        if i == 0 and not whole:
            continue
        value = staying * row + along * beside(q, row)
        if i:
            value = value + across * rows[i - 1]
        out.append(seas[i] * value)
    return out


def edges(q, coefficients, rows, seas, number):
    found = [rows[-1]]
    rows, seas = rows[-number:], seas[-number:]
    for _ in range(number - 1):
        rows = substep(q, coefficients, rows, seas, False)
        seas = seas[1:]
        found.append(rows[-1])
    return found


def upstream_part(q, coefficients, seas, beside_second_sea, halo):
    staying, along, across = coefficients
    first = seas[0] * (across * halo[0])
    beside_first = beside(q, first)
    second = seas[1] * (across * first)
    beside_second = beside_second_sea * (across * beside_first)
    first = seas[0] * (staying * first + along * beside_first + across * halo[1])
    third = seas[2] * (across * second)
    second = seas[1] * (staying * second + along * beside_second + across * first)
    first = seas[0] * (staying * first + along * beside(q, first))
    return [first, second, third]


def half_at(q, i, block):
    return pl.ds(block * HALF + (q % 2) * ARC_ROWS + i * SUB, SUB)


def send(block, slot, found, odd, cross_ref, inner_ref):
    for i in range(ARC):
        for q in range(2):
            at = half_at(q, i, block)
            north, south = found[q, i], found[q + 2, i]
            if cross_ref is not None:
                cross_ref[slot[0], at, :] = jnp.where(odd, north, south)
            if inner_ref is not None:
                inner_ref[slot[1], at, :] = jnp.where(odd, south, north)


def receive(q, i, block, slot, odd, cross_ref, inner_ref):
    at = half_at(q, i, block)
    cross, inner = cross_ref[slot[0], at, :], inner_ref[slot[1], at, :]
    return jnp.where(odd, inner, cross) if NORTH[q] else jnp.where(odd, cross, inner)


def spread(ref, r):
    row = ref[pl.ds(r, 1), :]
    return jnp.broadcast_to(row.astype(jnp.float32), (SUB, row.shape[1]))


def spread_all(ref, count):
    return [spread(ref, r) for r in range(count)]


def reader(row_refs):
    if len(row_refs) == 1:
        whole, = row_refs
        return whole.shape, lambda r, at: whole[r, at, :]
    edge, middle = row_refs
    count = middle.shape[0] + 2

    def row(r, at):
        if r == 0:
            return edge[0, at, :]
        if r == count - 1:
            return edge[1, at, :]
        return middle[r - 1, at, :]

    return (count,) + tuple(middle.shape[1:]), row


def early_messages(block, row, count, seas, trig_ref, odd, cross_ref):
    found = {}
    for q, i, at, coefficients in tiles(trig_ref, block):
        rows = flow(q, [row(r, at) for r in range(count)])
        found[q, i] = edges(q, coefficients, rows, flow(q, seas), SUBSTEPS - 1)
    for j in range(SUBSTEPS - 1):
        send(block, (j,), {key: f[j] for key, f in found.items()}, odd, cross_ref, None)


def first_kernel(odd_ref, f_hbm, sea_hbm, trig_hbm, f_ref, sea_ref, trig_ref, cross_ref, raw_ref, sem, block_sem):
    count, _, width = f_ref.shape

    def block_copy(block):
        at = pl.ds(pl.multiple_of(block * BLOCK, BLOCK), BLOCK)
        return pltpu.make_async_copy(f_hbm.at[:, at, :], raw_ref.at[:, at, :], block_sem.at[block])

    small = [pltpu.make_async_copy(sea_hbm, sea_ref, sem.at[0]), pltpu.make_async_copy(trig_hbm, trig_ref, sem.at[1])]
    for copy in small:
        copy.start()
    for block in range(BLOCKS):
        block_copy(block).start()
    for copy in small:
        copy.wait()
    iota = sublanes(width)
    odd = odd_ref[0] == 1
    seas = spread_all(sea_ref, count)

    def body(block, carry):
        block_copy(block).wait()
        put_in_order(block, lambda r, at: raw_ref[r, at, :], f_ref, range(count), iota)
        early_messages(block, lambda r, at: f_ref[r, at, :], count, seas, trig_ref, odd, cross_ref)
        return carry

    lax.fori_loop(0, BLOCKS, body, 0)


def put_in_order(block, read, out_ref, rows, iota):
    for r in rows:
        for t in range(BLOCK // SUB):
            tile = reorder(lambda index: read(r, pl.ds(block * BLOCK + index * SUB, SUB)), ORDER, t, iota)
            out_ref[r, pl.ds(block * BLOCK + t * SUB, SUB), :] = tile


def late_kernel(odd_ref, sea_ref, trig_ref, *refs):
    (count, _, width), row = reader(refs[:-2])
    cross_ref, inner_ref = refs[-2:]
    odd = odd_ref[0] == 1
    seas = spread_all(sea_ref, count)

    def body(block, carry):
        found = {}
        for q, i, at, coefficients in tiles(trig_ref, block):
            rows = flow(q, [row(r, at) for r in range(count)])
            found[q, i] = edges(q, coefficients, rows, flow(q, seas), SUBSTEPS)
        for j in range(SUBSTEPS):
            last = j == SUBSTEPS - 1
            send(block, (0, j), {key: f[j] for key, f in found.items()}, odd, cross_ref if last else None, inner_ref)
        return carry

    lax.fori_loop(0, BLOCKS, body, 0)


def local_kernel(sea_ref, trig_ref, *refs):
    (count, _, width), row = reader(refs[:-1])
    local_ref = refs[-1]
    seas = spread_all(sea_ref, count)

    def body(block, carry):
        for q, i, at, coefficients in tiles(trig_ref, block):
            rows = flow(q, [row(r, at) for r in range(count)])
            for _ in range(SUBSTEPS):
                rows = substep(q, coefficients, rows, flow(q, seas), True)
            for r, value in enumerate(flow(q, rows)):
                local_ref[r, at, :] = value
        return carry

    lax.fori_loop(0, BLOCKS, body, 0)


def lanes(ref, rows):
    return jnp.concatenate([ref[r:r + 1, :].astype(jnp.float32) for r in rows], axis=1)


def source_steps(rows, sums, sea_ref, ice_ref, wind_ref, matrix_ref, f_acc, b_acc, ready=None):
    comps = f_acc.shape[0]
    sea, gain = lanes(sea_ref, rows), source_rate * lanes(wind_ref, rows)
    energy = jnp.concatenate([jnp.sum(s, axis=0, keepdims=True) for s in sums], axis=1)
    chunk = comps // CHUNKS
    for s in range(SRC_SUB):
        scale = sea / (1.0 + (damping / comps) * energy)
        energy = jnp.zeros_like(energy)
        if s + 1 == SRC_SUB:
            scale = scale * (1.0 - 0.5 * lanes(ice_ref, rows))
        for c in range(comps // chunk):
            at = pl.ds(c * chunk, chunk)
            growth = jnp.dot(matrix_ref[at, :], b_acc[s % 2], preferred_element_type=jnp.float32)
            value = (f_acc[at, :] + gain * growth) * scale
            f_acc[at, :] = value
            if s + 1 < SRC_SUB:
                b_acc[(s + 1) % 2, at, :] = value.astype(jnp.bfloat16)
                energy = energy + jnp.sum(value * value, axis=0, keepdims=True)
            elif ready is not None:
                ready(c, at)


def hold(block, column, read, iota, f_acc, b_acc, total):
    width = iota.shape[1]
    columns = slice(column * width, (column + 1) * width)
    for t in range(0, BLOCK // SUB, 2):
        pair = [reorder(read, INVERSE, t + k, iota) for k in range(2)]
        both = jnp.concatenate(pair, axis=0)
        at = pl.ds(block * BLOCK + t * SUB, 2 * SUB)
        f_acc[at, columns] = both
        b_acc[0, at, columns] = both.astype(jnp.bfloat16)
        total = total + pair[0] * pair[0] + pair[1] * pair[1]
    return total


def middle_kernel(last, odd_ref, sea_ref, ice_ref, wind_ref, trig_ref, matrix_ref, cross_ref, inner_ref, local_ref,
                  middle_ref, edge_ref, f_acc, b_acc, moved):
    count, _, width = local_ref.shape
    iota = sublanes(width)
    odd = odd_ref[0] == 1
    seas = spread_all(sea_ref, count)
    beside_seas = [beside(q, flow(q, seas)[1]) for q in range(QUADRANTS)]
    between_rows = range(1, count - 1)

    def advance(block, sums):
        for q, i, at, coefficients in tiles(trig_ref, block):
            halo = [receive(q, i, block, (j, j), odd, cross_ref, inner_ref) for j in range(SUBSTEPS - 1)]
            rows = upstream_part(q, coefficients, flow(q, seas), beside_seas[q], halo)
            rows = flow(q, rows + [0.0] * (count - len(rows)))
            rows = [local_ref[r, at, :] + value for r, value in enumerate(rows)]
            edge_ref[0, at, :], edge_ref[1, at, :] = rows[0], rows[-1]
            for r in between_rows:
                moved[r - 1, at, :] = rows[r]
        return tuple(
            hold(block, i, lambda t: moved[i, pl.ds(block * BLOCK + t * SUB, SUB), :], iota, f_acc, b_acc, total)
            for i, total in enumerate(sums))

    zero = jnp.zeros((SUB, width), jnp.float32)
    sums = lax.fori_loop(0, BLOCKS, advance, (zero,) * len(between_rows))
    source_steps(between_rows, sums, sea_ref, ice_ref, wind_ref, matrix_ref, f_acc, b_acc)
    if last:
        for i in range(count - 2):
            middle_ref[i] = f_acc[:, i * width:(i + 1) * width]
        return

    def finish(block, carry):
        put_in_order(block, lambda r, at: f_acc[at, r * width:(r + 1) * width], middle_ref, range(count - 2), iota)
        return carry

    lax.fori_loop(0, BLOCKS, finish, 0)


def edge_kernel(last, odd_ref, sea_ref, ice_ref, wind_ref, trig_ref, matrix_ref, cross_in, inner_in, part_ref, middle_ref, *refs):
    if last:
        out_ref, f_acc, b_acc, moved, sem = refs
    else:
        out_ref, cross_ref, f_acc, b_acc, moved = refs
    count, width = middle_ref.shape[0] + 2, middle_ref.shape[2]
    iota = sublanes(width)
    odd = odd_ref[0] == 1
    seas = spread_all(sea_ref, count)
    edge_rows = (0, count - 1)
    if last:
        copies = [pltpu.make_async_copy(middle_ref, out_ref.at[pl.ds(1, count - 2)], sem.at[2 * CHUNKS])]
        copies[0].start()

    def advance(block, sums):
        for q, i, at, (_, _, across) in tiles(trig_ref, block):
            halo = receive(q, i, block, (0, SUBSTEPS - 1), odd, cross_in, inner_in)
            first, other = flow(q, (0, 1))
            moved[first, at, :] = part_ref[first, at, :] + flow(q, seas)[0] * (across * halo)
            moved[other, at, :] = part_ref[other, at, :]
        return tuple(
            hold(block, i, lambda t: moved[i, pl.ds(block * BLOCK + t * SUB, SUB), :], iota, f_acc, b_acc, total)
            for i, total in enumerate(sums))

    zero = jnp.zeros((SUB, width), jnp.float32)
    sums = lax.fori_loop(0, BLOCKS, advance, (zero, zero))
    if last:
        def ready(c, at):
            for i, r in enumerate(edge_rows):
                columns = pl.ds(i * width, width)
                copy = pltpu.make_async_copy(f_acc.at[at, columns], out_ref.at[r, at, :], sem.at[2 * c + i])
                copy.start()
                copies.append(copy)

        source_steps(edge_rows, sums, sea_ref, ice_ref, wind_ref, matrix_ref, f_acc, b_acc, ready)
        for copy in copies:
            copy.wait()
        return
    source_steps(edge_rows, sums, sea_ref, ice_ref, wind_ref, matrix_ref, f_acc, b_acc)
    _, row = reader((out_ref, middle_ref))

    def finish(block, carry):
        put_in_order(block, lambda r, at: f_acc[at, r * width:(r + 1) * width], out_ref, range(2), iota)
        early_messages(block, row, count, seas, trig_ref, odd, cross_ref)
        return carry

    lax.fori_loop(0, BLOCKS, finish, 0)


def on_device(spectrum, sea_mask, ice_mask, wind, source_matrix):
    size = lax.axis_size("comp")
    comps, count, width = spectrum.shape
    assert comps == K and count >= SUBSTEPS and size % 2 == 0
    odd = (lax.axis_index("comp") % 2).astype(jnp.int32).reshape(1)
    f = jnp.transpose(spectrum, (1, 0, 2))
    trig = pattern()
    outer_pairs = [(i, i + 1) for i in range(1, size - 1, 2)]
    inner_pairs = [(i, i + 1) for i in range(0, size, 2)]

    def swap(value, pairs):
        return lax.ppermute(value, "comp", pairs + [(j, i) for i, j in pairs])

    vmem = pl.BlockSpec(memory_space=pltpu.VMEM)
    hbm = pl.BlockSpec(memory_space=pltpu.HBM)
    dma = pltpu.SemaphoreType.DMA

    def call(kernel, name, args, outs, scratch_rows=0, scratch=(), in_space=vmem, out_space=vmem, scalar=True, cost=0):
        scratch = list(scratch)
        if scratch_rows:
            scratch = [pltpu.VMEM((K, scratch_rows * width), jnp.float32),
                       pltpu.VMEM((2, K, scratch_rows * width), jnp.bfloat16),
                       pltpu.VMEM((scratch_rows, K, width), jnp.float32)] + scratch
        outs = [out if hasattr(out, "dtype") else jax.ShapeDtypeStruct(out, jnp.float32) for out in outs]
        return pl.pallas_call(
            kernel, out_shape=outs, name=name,
            in_specs=[pl.BlockSpec(memory_space=pltpu.SMEM)] * scalar + [in_space] * len(args),
            out_specs=[out_space] * len(outs), scratch_shapes=scratch,
            cost_estimate=pl.CostEstimate(flops=cost, bytes_accessed=0, transcendentals=0) if cost else None,
            compiler_params=pltpu.CompilerParams(vmem_limit_bytes=24 * 1024 * 1024),
        )(*((odd,) if scalar else ()), *args)

    def message(slots):
        return (slots, K // 2, width)

    whole = jax.ShapeDtypeStruct((count, K, width), jnp.float32)
    operands = [pltpu.with_memory_space_constraint(x, pltpu.HBM) for x in (f, sea_mask, trig)]
    f, sea, trig, cross = call(
        first_kernel, "first_edges", operands, [whole, sea_mask, trig, message(SUBSTEPS - 1)],
        scratch=[pltpu.VMEM(whole.shape, jnp.float32), dma((2,)), dma((BLOCKS,))], in_space=hbm)
    rows = (f,)
    masks = (sea, ice_mask, wind, trig, source_matrix)
    for step in range(STEPS):
        last = step == STEPS - 1
        cross = swap(cross, outer_pairs)
        cross_late, inner = call(late_kernel, "late_edges", (sea, trig) + rows, [message(1), message(SUBSTEPS)])
        cross_late = swap(cross_late, outer_pairs)
        inner = swap(inner, inner_pairs)
        local, = call(local_kernel, "local_rows", (sea, trig) + rows, [whole], scalar=False, cost=30000000000)
        middle, part = call(functools.partial(middle_kernel, last), "middle_rows", masks + (cross, inner, local),
                            [(count - 2, K, width), (2, K, width)], count - 2)
        outs = [whole] if last else [(2, K, width), message(SUBSTEPS - 1)]
        result = call(functools.partial(edge_kernel, last), "edge_rows", masks + (cross_late, inner, part, middle), outs, 2,
                      scratch=[dma((2 * CHUNKS + 1,))] if last else (), out_space=hbm if last else vmem)
        if last:
            return jnp.transpose(result[0], (1, 0, 2))
        rows, cross = (result[0], middle), result[1]


def solution(mesh):
    return jax.shard_map(
        on_device,
        mesh=mesh,
        in_specs=(
            P(None, ("grp", "comp"), None),
            P(("grp", "comp"), None),
            P(("grp", "comp"), None),
            P(("grp", "comp"), None),
            P(),
        ),
        out_specs=P(None, ("grp", "comp"), None),
        check_vma=False,
    )
```

```python
import functools

import jax
import jax.numpy as jnp
import numpy as np
from jax import lax
from jax.experimental import pallas as pl
from jax.experimental.pallas import tpu as pltpu
from jax.sharding import PartitionSpec as P

NDIR = 36
NFREQ = 32
K = 1152
STEPS = 2
SUBSTEPS = 3
SRC_SUB = 3

source_rate = 0.5
damping = 0.5

SUB = 8
QUADRANTS = 4
ARC = NDIR // QUADRANTS
ARC_ROWS = SUB * ARC
BLOCK = QUADRANTS * ARC_ROWS
BLOCKS = K // BLOCK
HALF = BLOCK // 2
CHUNKS = 4
EAST = (True, False, False, True)
NORTH = (True, True, False, False)


def source_row(row):
    quadrant, rest = divmod(row, ARC_ROWS)
    frequency, direction = divmod(rest, ARC)
    return frequency * NDIR + quadrant * ARC + direction


ORDER = [source_row(row) for row in range(BLOCK)]
INVERSE = [ORDER.index(row) for row in range(BLOCK)]


def reorder(read, order, tile, iota):
    pieces = {}
    for to, row in enumerate(order[tile * SUB:(tile + 1) * SUB]):
        pieces.setdefault((row // SUB, (to - row) % SUB), []).append(to)
    out = None
    for (index, shift), rows in pieces.items():
        value = read(index)
        if shift:
            value = pltpu.roll(value, shift, 0)
        out = value if out is None else jnp.where((iota >= rows[0]) & (iota <= rows[-1]), value, out)
    return out


def pattern():
    row = np.arange(ARC_ROWS)
    theta = 2.0 * np.pi * (row % ARC + 0.5) / NDIR
    slower = 0.6 * 0.65 / (NFREQ - 1) * (row // ARC)
    table = np.stack([np.cos(theta), np.sin(theta), slower]).astype(np.float32)
    return jnp.asarray(np.ascontiguousarray(np.broadcast_to(table[:, :, None], (3, ARC_ROWS, 128))))


def sublanes(width):
    return lax.broadcasted_iota(jnp.int32, (SUB, width), 0)


def block_parts(trig_ref, block):
    frequency = (block * SUB).astype(jnp.float32)
    fastest = 0.6 * (0.35 + (0.65 / (NFREQ - 1)) * ((NFREQ - 1) - frequency))
    cosine, sine, slower = (trig_ref[i].reshape(ARC, SUB, -1) for i in range(3))
    one, other = (fastest - slower) * cosine, (fastest - slower) * sine
    staying = 1.0 - one - other
    for q in range(QUADRANTS):
        at = pl.ds(block * BLOCK + q * ARC_ROWS, ARC_ROWS)
        yield q, at, (staying, one, other) if q % 2 == 0 else (staying, other, one)


def get(ref, r, at):
    return ref[r, at, :].reshape(ARC, SUB, -1)


def put(ref, r, at, value):
    ref[r, at, :] = value.reshape(ARC_ROWS, -1)


def beside(q, value):
    last = value.ndim - 1
    return pltpu.roll(value, 1 if EAST[q] else value.shape[last] - 1, last)


def flow(q, rows):
    return list(rows) if NORTH[q] else list(rows)[::-1]


def substep(q, coefficients, rows, seas, whole):
    staying, along, across = coefficients
    out = []
    for i, row in enumerate(rows):
        if i == 0 and not whole:
            continue
        value = staying * row + along * beside(q, row)
        if i:
            value = value + across * rows[i - 1]
        out.append(seas[i] * value)
    return out


def edges(q, coefficients, rows, seas, number):
    found = [rows[-1]]
    rows, seas = rows[-number:], seas[-number:]
    for _ in range(number - 1):
        rows = substep(q, coefficients, rows, seas, False)
        seas = seas[1:]
        found.append(rows[-1])
    return found


def upstream_part(q, coefficients, seas, beside_second_sea, halo):
    staying, along, across = coefficients
    first = seas[0] * (across * halo[0])
    beside_first = beside(q, first)
    second = seas[1] * (across * first)
    beside_second = beside_second_sea * (across * beside_first)
    first = seas[0] * (staying * first + along * beside_first + across * halo[1])
    third = seas[2] * (across * second)
    second = seas[1] * (staying * second + along * beside_second + across * first)
    first = seas[0] * (staying * first + along * beside(q, first))
    return [first, second, third]


def half_at(q, block):
    return pl.ds(block * HALF + (q % 2) * ARC_ROWS, ARC_ROWS)


def send(block, slot, found, odd, cross_ref, inner_ref):
    for q in range(2):
        north, south = found[q], found[q + 2]
        if cross_ref is not None:
            put(cross_ref, slot[0], half_at(q, block), jnp.where(odd, north, south))
        if inner_ref is not None:
            put(inner_ref, slot[1], half_at(q, block), jnp.where(odd, south, north))


def receive(q, block, slot, odd, cross_ref, inner_ref):
    at = half_at(q, block)
    cross, inner = get(cross_ref, slot[0], at), get(inner_ref, slot[1], at)
    return jnp.where(odd, inner, cross) if NORTH[q] else jnp.where(odd, cross, inner)


def spread(ref, r):
    row = ref[pl.ds(r, 1), :]
    return jnp.broadcast_to(row.astype(jnp.float32), (SUB, row.shape[1]))


def spread_all(ref, count):
    return [spread(ref, r) for r in range(count)]


def reader(row_refs):
    if len(row_refs) == 1:
        whole, = row_refs
        return whole.shape, lambda r, at: get(whole, r, at)
    edge, middle = row_refs
    count = middle.shape[0] + 2

    def row(r, at):
        if r == 0:
            return get(edge, 0, at)
        if r == count - 1:
            return get(edge, 1, at)
        return get(middle, r - 1, at)

    return (count,) + tuple(middle.shape[1:]), row


def early_messages(block, row, count, seas, trig_ref, odd, cross_ref):
    found = []
    for q, at, coefficients in block_parts(trig_ref, block):
        rows = flow(q, [row(r, at) for r in range(count)])
        found.append(edges(q, coefficients, rows, flow(q, seas), SUBSTEPS - 1))
    for j in range(SUBSTEPS - 1):
        send(block, (j,), [f[j] for f in found], odd, cross_ref, None)


def first_kernel(odd_ref, f_hbm, sea_hbm, trig_hbm, f_ref, sea_ref, trig_ref, cross_ref, raw_ref, sem, block_sem):
    count, _, width = f_ref.shape

    def block_copy(block):
        at = pl.ds(pl.multiple_of(block * BLOCK, BLOCK), BLOCK)
        return pltpu.make_async_copy(f_hbm.at[:, at, :], raw_ref.at[:, at, :], block_sem.at[block])

    small = [pltpu.make_async_copy(sea_hbm, sea_ref, sem.at[0]), pltpu.make_async_copy(trig_hbm, trig_ref, sem.at[1])]
    for copy in small:
        copy.start()
    for block in range(BLOCKS):
        block_copy(block).start()
    for copy in small:
        copy.wait()
    iota = sublanes(width)
    odd = odd_ref[0] == 1
    seas = spread_all(sea_ref, count)

    def body(block, carry):
        block_copy(block).wait()
        put_in_order(block, lambda r, at: raw_ref[r, at, :], f_ref, range(count), iota)
        early_messages(block, lambda r, at: get(f_ref, r, at), count, seas, trig_ref, odd, cross_ref)
        return carry

    lax.fori_loop(0, BLOCKS, body, 0)


def put_in_order(block, read, out_ref, rows, iota):
    for r in rows:
        for t in range(BLOCK // SUB):
            tile = reorder(lambda index: read(r, pl.ds(block * BLOCK + index * SUB, SUB)), ORDER, t, iota)
            out_ref[r, pl.ds(block * BLOCK + t * SUB, SUB), :] = tile


def late_kernel(odd_ref, sea_ref, trig_ref, *refs):
    (count, _, width), row = reader(refs[:-2])
    cross_ref, inner_ref = refs[-2:]
    odd = odd_ref[0] == 1
    seas = spread_all(sea_ref, count)

    def body(block, carry):
        found = []
        for q, at, coefficients in block_parts(trig_ref, block):
            rows = flow(q, [row(r, at) for r in range(count)])
            found.append(edges(q, coefficients, rows, flow(q, seas), SUBSTEPS))
        for j in range(SUBSTEPS):
            last = j == SUBSTEPS - 1
            send(block, (0, j), [f[j] for f in found], odd, cross_ref if last else None, inner_ref)
        return carry

    lax.fori_loop(0, BLOCKS, body, 0)


def local_kernel(sea_ref, trig_ref, *refs):
    (count, _, width), row = reader(refs[:-1])
    local_ref = refs[-1]
    seas = spread_all(sea_ref, count)

    def body(block, carry):
        for q, at, coefficients in block_parts(trig_ref, block):
            rows = flow(q, [row(r, at) for r in range(count)])
            for _ in range(SUBSTEPS):
                rows = substep(q, coefficients, rows, flow(q, seas), True)
            for r, value in enumerate(flow(q, rows)):
                put(local_ref, r, at, value)
        return carry

    lax.fori_loop(0, BLOCKS, body, 0)


def lanes(ref, rows):
    return jnp.concatenate([ref[r:r + 1, :].astype(jnp.float32) for r in rows], axis=1)


def source_steps(rows, sums, sea_ref, ice_ref, wind_ref, matrix_ref, f_acc, b_acc, ready=None):
    comps = f_acc.shape[0]
    sea, gain = lanes(sea_ref, rows), source_rate * lanes(wind_ref, rows)
    energy = jnp.concatenate([jnp.sum(s, axis=0, keepdims=True) for s in sums], axis=1)
    chunk = comps // CHUNKS
    for s in range(SRC_SUB):
        scale = sea / (1.0 + (damping / comps) * energy)
        energy = jnp.zeros_like(energy)
        if s + 1 == SRC_SUB:
            scale = scale * (1.0 - 0.5 * lanes(ice_ref, rows))
        for c in range(comps // chunk):
            at = pl.ds(c * chunk, chunk)
            growth = jnp.dot(matrix_ref[at, :], b_acc[s % 2], preferred_element_type=jnp.float32)
            value = (f_acc[at, :] + gain * growth) * scale
            f_acc[at, :] = value
            if s + 1 < SRC_SUB:
                b_acc[(s + 1) % 2, at, :] = value.astype(jnp.bfloat16)
                energy = energy + jnp.sum(value * value, axis=0, keepdims=True)
            elif ready is not None:
                ready(c, at)


def hold(block, column, read, iota, f_acc, b_acc, total):
    width = iota.shape[1]
    columns = slice(column * width, (column + 1) * width)
    for t in range(0, BLOCK // SUB, 2):
        pair = [reorder(read, INVERSE, t + k, iota) for k in range(2)]
        both = jnp.concatenate(pair, axis=0)
        at = pl.ds(block * BLOCK + t * SUB, 2 * SUB)
        f_acc[at, columns] = both
        b_acc[0, at, columns] = both.astype(jnp.bfloat16)
        total = total + pair[0] * pair[0] + pair[1] * pair[1]
    return total


def middle_kernel(last, odd_ref, sea_ref, ice_ref, wind_ref, trig_ref, matrix_ref, cross_ref, inner_ref, local_ref,
                  middle_ref, edge_ref, f_acc, b_acc, moved):
    count, _, width = local_ref.shape
    iota = sublanes(width)
    odd = odd_ref[0] == 1
    seas = spread_all(sea_ref, count)
    beside_seas = [beside(q, flow(q, seas)[1]) for q in range(QUADRANTS)]
    between_rows = range(1, count - 1)

    def advance(block, sums):
        for q, at, coefficients in block_parts(trig_ref, block):
            halo = [receive(q, block, (j, j), odd, cross_ref, inner_ref) for j in range(SUBSTEPS - 1)]
            rows = upstream_part(q, coefficients, flow(q, seas), beside_seas[q], halo)
            rows = flow(q, rows + [0.0] * (count - len(rows)))
            rows = [get(local_ref, r, at) + value for r, value in enumerate(rows)]
            put(edge_ref, 0, at, rows[0])
            put(edge_ref, 1, at, rows[-1])
            for r in between_rows:
                put(moved, r - 1, at, rows[r])
        return tuple(
            hold(block, i, lambda t: moved[i, pl.ds(block * BLOCK + t * SUB, SUB), :], iota, f_acc, b_acc, total)
            for i, total in enumerate(sums))

    zero = jnp.zeros((SUB, width), jnp.float32)
    sums = lax.fori_loop(0, BLOCKS, advance, (zero,) * len(between_rows))
    source_steps(between_rows, sums, sea_ref, ice_ref, wind_ref, matrix_ref, f_acc, b_acc)
    if last:
        for i in range(count - 2):
            middle_ref[i] = f_acc[:, i * width:(i + 1) * width]
        return

    def finish(block, carry):
        put_in_order(block, lambda r, at: f_acc[at, r * width:(r + 1) * width], middle_ref, range(count - 2), iota)
        return carry

    lax.fori_loop(0, BLOCKS, finish, 0)


def edge_kernel(last, odd_ref, sea_ref, ice_ref, wind_ref, trig_ref, matrix_ref, cross_in, inner_in, part_ref, middle_ref, *refs):
    if last:
        out_ref, f_acc, b_acc, moved, sem = refs
    else:
        out_ref, cross_ref, f_acc, b_acc, moved = refs
    count, width = middle_ref.shape[0] + 2, middle_ref.shape[2]
    iota = sublanes(width)
    odd = odd_ref[0] == 1
    seas = spread_all(sea_ref, count)
    edge_rows = (0, count - 1)
    if last:
        copies = [pltpu.make_async_copy(middle_ref, out_ref.at[pl.ds(1, count - 2)], sem.at[2 * CHUNKS])]
        copies[0].start()

    def advance(block, sums):
        for q, at, (_, _, across) in block_parts(trig_ref, block):
            halo = receive(q, block, (0, SUBSTEPS - 1), odd, cross_in, inner_in)
            first, other = flow(q, (0, 1))
            put(moved, first, at, get(part_ref, first, at) + flow(q, seas)[0] * (across * halo))
            put(moved, other, at, get(part_ref, other, at))
        return tuple(
            hold(block, i, lambda t: moved[i, pl.ds(block * BLOCK + t * SUB, SUB), :], iota, f_acc, b_acc, total)
            for i, total in enumerate(sums))

    zero = jnp.zeros((SUB, width), jnp.float32)
    sums = lax.fori_loop(0, BLOCKS, advance, (zero, zero))
    if last:
        def ready(c, at):
            for i, r in enumerate(edge_rows):
                columns = pl.ds(i * width, width)
                copy = pltpu.make_async_copy(f_acc.at[at, columns], out_ref.at[r, at, :], sem.at[2 * c + i])
                copy.start()
                copies.append(copy)

        source_steps(edge_rows, sums, sea_ref, ice_ref, wind_ref, matrix_ref, f_acc, b_acc, ready)
        for copy in copies:
            copy.wait()
        return
    source_steps(edge_rows, sums, sea_ref, ice_ref, wind_ref, matrix_ref, f_acc, b_acc)
    _, row = reader((out_ref, middle_ref))

    def finish(block, carry):
        put_in_order(block, lambda r, at: f_acc[at, r * width:(r + 1) * width], out_ref, range(2), iota)
        early_messages(block, row, count, seas, trig_ref, odd, cross_ref)
        return carry

    lax.fori_loop(0, BLOCKS, finish, 0)


def on_device(spectrum, sea_mask, ice_mask, wind, source_matrix):
    size = lax.axis_size("comp")
    comps, count, width = spectrum.shape
    assert comps == K and count >= SUBSTEPS and size % 2 == 0
    odd = (lax.axis_index("comp") % 2).astype(jnp.int32).reshape(1)
    f = jnp.transpose(spectrum, (1, 0, 2))
    trig = pattern()
    outer_pairs = [(i, i + 1) for i in range(1, size - 1, 2)]
    inner_pairs = [(i, i + 1) for i in range(0, size, 2)]

    def swap(value, pairs):
        return lax.ppermute(value, "comp", pairs + [(j, i) for i, j in pairs])

    vmem = pl.BlockSpec(memory_space=pltpu.VMEM)
    hbm = pl.BlockSpec(memory_space=pltpu.HBM)
    dma = pltpu.SemaphoreType.DMA

    def call(kernel, name, args, outs, scratch_rows=0, scratch=(), in_space=vmem, out_space=vmem, scalar=True, cost=0):
        scratch = list(scratch)
        if scratch_rows:
            scratch = [pltpu.VMEM((K, scratch_rows * width), jnp.float32),
                       pltpu.VMEM((2, K, scratch_rows * width), jnp.bfloat16),
                       pltpu.VMEM((scratch_rows, K, width), jnp.float32)] + scratch
        outs = [out if hasattr(out, "dtype") else jax.ShapeDtypeStruct(out, jnp.float32) for out in outs]
        return pl.pallas_call(
            kernel, out_shape=outs, name=name,
            in_specs=[pl.BlockSpec(memory_space=pltpu.SMEM)] * scalar + [in_space] * len(args),
            out_specs=[out_space] * len(outs), scratch_shapes=scratch,
            cost_estimate=pl.CostEstimate(flops=cost, bytes_accessed=0, transcendentals=0) if cost else None,
            compiler_params=pltpu.CompilerParams(vmem_limit_bytes=24 * 1024 * 1024),
        )(*((odd,) if scalar else ()), *args)

    def message(slots):
        return (slots, K // 2, width)

    whole = jax.ShapeDtypeStruct((count, K, width), jnp.float32)
    operands = [pltpu.with_memory_space_constraint(x, pltpu.HBM) for x in (f, sea_mask, trig)]
    f, sea, trig, cross = call(
        first_kernel, "first_edges", operands, [whole, sea_mask, trig, message(SUBSTEPS - 1)],
        scratch=[pltpu.VMEM(whole.shape, jnp.float32), dma((2,)), dma((BLOCKS,))], in_space=hbm)
    rows = (f,)
    masks = (sea, ice_mask, wind, trig, source_matrix)
    for step in range(STEPS):
        last = step == STEPS - 1
        cross = swap(cross, outer_pairs)
        cross_late, inner = call(late_kernel, "late_edges", (sea, trig) + rows, [message(1), message(SUBSTEPS)])
        cross_late = swap(cross_late, outer_pairs)
        inner = swap(inner, inner_pairs)
        local, = call(local_kernel, "local_rows", (sea, trig) + rows, [whole], scalar=False, cost=30000000000)
        middle, part = call(functools.partial(middle_kernel, last), "middle_rows", masks + (cross, inner, local),
                            [(count - 2, K, width), (2, K, width)], count - 2)
        outs = [whole] if last else [(2, K, width), message(SUBSTEPS - 1)]
        result = call(functools.partial(edge_kernel, last), "edge_rows", masks + (cross_late, inner, part, middle), outs, 2,
                      scratch=[dma((2 * CHUNKS + 1,))] if last else (), out_space=hbm if last else vmem)
        if last:
            return jnp.transpose(result[0], (1, 0, 2))
        rows, cross = (result[0], middle), result[1]


def solution(mesh):
    return jax.shard_map(
        on_device,
        mesh=mesh,
        in_specs=(
            P(None, ("grp", "comp"), None),
            P(("grp", "comp"), None),
            P(("grp", "comp"), None),
            P(("grp", "comp"), None),
            P(),
        ),
        out_specs=P(None, ("grp", "comp"), None),
        check_vma=False,
    )
```

```python
import functools

import jax
import jax.numpy as jnp
import numpy as np
from jax import lax
from jax.experimental import pallas as pl
from jax.experimental.pallas import tpu as pltpu
from jax.sharding import PartitionSpec as P

NDIR = 36
NFREQ = 32
K = 1152
STEPS = 2
SUBSTEPS = 3
SRC_SUB = 3

source_rate = 0.5
damping = 0.5

SUB = 8
QUADRANTS = 4
ARC = NDIR // QUADRANTS
ARC_ROWS = SUB * ARC
BLOCK = QUADRANTS * ARC_ROWS
BLOCKS = K // BLOCK
HALF = BLOCK // 2
CHUNKS = 4
EAST = (True, False, False, True)
INWARD = (True, True, False, False)
NEAR = SUBSTEPS - 1


def source_row(row):
    quadrant, rest = divmod(row, ARC_ROWS)
    frequency, direction = divmod(rest, ARC)
    return frequency * NDIR + quadrant * ARC + direction


ORDER = [source_row(row) for row in range(BLOCK)]
INVERSE = [ORDER.index(row) for row in range(BLOCK)]


def reorder(read, order, tile, iota):
    pieces = {}
    for to, row in enumerate(order[tile * SUB:(tile + 1) * SUB]):
        pieces.setdefault((row // SUB, (to - row) % SUB), []).append(to)
    out = None
    for (index, shift), rows in pieces.items():
        value = read(index)
        if shift:
            value = pltpu.roll(value, shift, 0)
        out = value if out is None else jnp.where((iota >= rows[0]) & (iota <= rows[-1]), value, out)
    return out


def pattern():
    row = np.arange(ARC_ROWS)
    theta = 2.0 * np.pi * (row % ARC + 0.5) / NDIR
    slower = 0.6 * 0.65 / (NFREQ - 1) * (row // ARC)
    table = np.stack([np.cos(theta), np.sin(theta), slower]).astype(np.float32)
    return jnp.asarray(np.ascontiguousarray(np.broadcast_to(table[:, :, None], (3, ARC_ROWS, 128))))


def sublanes(width):
    return lax.broadcasted_iota(jnp.int32, (SUB, width), 0)


def counted(odd, i, count):
    return odd * (count - 1) + (1 - 2 * odd) * i


def tile_at(odd, block, index):
    q, i = divmod(index, ARC)
    return pl.ds(pl.multiple_of(block * BLOCK + counted(odd, q, QUADRANTS) * ARC_ROWS + i * SUB, SUB), SUB)


def quadrant_at(block, q):
    return pl.ds(block * BLOCK + q * ARC_ROWS, ARC_ROWS)


def half_at(block, q):
    return pl.ds(block * HALF + (q if INWARD[q] else QUADRANTS - 1 - q) * ARC_ROWS, ARC_ROWS)


def block_coefficients(trig_ref, block):
    frequency = (block * SUB).astype(jnp.float32)
    fastest = 0.6 * (0.35 + (0.65 / (NFREQ - 1)) * ((NFREQ - 1) - frequency))
    cosine, sine, slower = (trig_ref[i].reshape(ARC, SUB, -1) for i in range(3))
    one, other = (fastest - slower) * cosine, (fastest - slower) * sine
    staying = 1.0 - one - other
    return [(staying, one, other) if q % 2 == 0 else (staying, other, one) for q in range(QUADRANTS)]


def get(ref, r, at):
    return ref[r, at, :].reshape(ARC, SUB, -1)


def put(ref, r, at, value):
    ref[r, at, :] = value.reshape(ARC_ROWS, -1)


def beside(q, value):
    last = value.ndim - 1
    return pltpu.roll(value, 1 if EAST[q] else value.shape[last] - 1, last)


def flow(q, rows):
    return list(rows) if INWARD[q] else list(rows)[::-1]


def substep(q, coefficients, rows, seas, whole):
    staying, along, across = coefficients
    out = []
    for i, row in enumerate(rows):
        if i == 0 and not whole:
            continue
        value = staying * row + along * beside(q, row)
        if i:
            value = value + across * rows[i - 1]
        out.append(seas[i] * value)
    return out


def edges(q, coefficients, rows, seas):
    found = [rows[-1]]
    rows, seas = rows[-SUBSTEPS:], seas[-SUBSTEPS:]
    for _ in range(SUBSTEPS - 1):
        rows = substep(q, coefficients, rows, seas, False)
        seas = seas[1:]
        found.append(rows[-1])
    return found


def first_two(q, coefficients, seas, halo):
    staying, along, across = coefficients
    first = seas[0] * (across * halo[0])
    beside_first = beside(q, first)
    second = seas[1] * (across * first)
    beside_second = beside(q, seas[1]) * (across * beside_first)
    first = seas[0] * (staying * first + along * beside_first + across * halo[1])
    after_two = second
    second = seas[1] * (staying * second + along * beside_second + across * first)
    first = seas[0] * (staying * first + along * beside(q, first) + across * halo[2])
    return first, second, after_two


def reader(row_refs):
    if len(row_refs) == 1:
        whole, = row_refs
        return whole.shape, lambda r, at: get(whole, r, at)
    near, far = row_refs
    shape = (NEAR + far.shape[0],) + tuple(far.shape[1:])
    return shape, lambda r, at: get(near, r, at) if r < NEAR else get(far, r - NEAR, at)


def spread_all(ref, count):
    return [jnp.broadcast_to(ref[r:r + 1, :].astype(jnp.float32), (SUB, ref.shape[1])) for r in range(count)]


def put_in_order(odd, block, read, out_ref, rows, iota):
    for r in rows:
        for t in range(BLOCK // SUB):
            tile = reorder(lambda index: read(r, pl.ds(block * BLOCK + index * SUB, SUB)), ORDER, t, iota)
            out_ref[r, tile_at(odd, block, t), :] = tile


def first_message(block, near_ref, cross_ref):
    for q in range(QUADRANTS):
        if not INWARD[q]:
            cross_ref[0, half_at(block, q), :] = near_ref[0, quadrant_at(block, q), :]


def first_kernel(odd_ref, f_hbm, sea_hbm, trig_hbm, f_ref, sea_ref, trig_ref, cross_ref, f_raw, sea_raw, trig_raw, sem, block_sem):
    count, _, width = f_ref.shape
    odd = odd_ref[0]

    def block_copy(block):
        at = pl.ds(pl.multiple_of(block * BLOCK, BLOCK), BLOCK)
        return pltpu.make_async_copy(f_hbm.at[:, at, :], f_raw.at[:, at, :], block_sem.at[block])

    small = [pltpu.make_async_copy(sea_hbm, sea_raw, sem.at[0]), pltpu.make_async_copy(trig_hbm, trig_raw, sem.at[1])]
    for block in range(BLOCKS):
        block_copy(block).start()
    for copy in small:
        copy.start()
    iota = sublanes(width)

    def body(block, carry):
        block_copy(block).wait()
        put_in_order(odd, block, lambda r, at: f_raw[counted(odd, r, count), at, :], f_ref, range(count), iota)
        first_message(block, f_ref, cross_ref)
        return carry

    lax.fori_loop(0, BLOCKS, body, 0)
    for copy in small:
        copy.wait()
    for r in range(count):
        sea_ref[r:r + 1, :] = sea_raw[pl.ds(counted(odd, r, count), 1), :]
    for i in range(2):
        trig_ref[i] = trig_raw[counted(odd, i, 2)]
    trig_ref[2] = trig_raw[2]


def late_kernel(sea_ref, trig_ref, *refs):
    cross_ref, inner_ref = refs[-2:]
    (count, _, _), row = reader(refs[:-2])
    seas = spread_all(sea_ref, count)

    def body(block, carry):
        for q, coefficients in enumerate(block_coefficients(trig_ref, block)):
            rows = flow(q, [row(r, quadrant_at(block, q)) for r in range(count)])
            found = edges(q, coefficients, rows, flow(q, seas))
            if INWARD[q]:
                for j in range(SUBSTEPS):
                    put(inner_ref, j, half_at(block, q), found[j])
            else:
                for j in range(1, SUBSTEPS):
                    put(cross_ref, j - 1, half_at(block, q), found[j])
        return carry

    lax.fori_loop(0, BLOCKS, body, 0)


def local_kernel(sea_ref, trig_ref, *refs):
    (count, _, _), row = reader(refs[:-1])
    local_ref = refs[-1]
    seas = spread_all(sea_ref, count)

    def body(block, carry):
        for q, coefficients in enumerate(block_coefficients(trig_ref, block)):
            at = quadrant_at(block, q)
            rows = flow(q, [row(r, at) for r in range(count)])
            for _ in range(SUBSTEPS):
                rows = substep(q, coefficients, rows, flow(q, seas), True)
            for r, value in enumerate(flow(q, rows)):
                put(local_ref, r, at, value)
        return carry

    lax.fori_loop(0, BLOCKS, body, 0)


def lanes(ref, rows):
    return jnp.concatenate([ref[pl.ds(r, 1), :].astype(jnp.float32) for r in rows], axis=1)


def source_steps(odd, rows, sums, sea_ref, ice_ref, wind_ref, matrix_ref, f_acc, b_acc, ready=None):
    comps, count = f_acc.shape[0], sea_ref.shape[0]
    there = [counted(odd, r, count) for r in rows]
    sea, gain, thaw = lanes(sea_ref, rows), source_rate * lanes(wind_ref, there), 1.0 - 0.5 * lanes(ice_ref, there)
    energy = jnp.concatenate([jnp.sum(s, axis=0, keepdims=True) for s in sums], axis=1)
    chunk = comps // CHUNKS
    for s in range(SRC_SUB):
        scale = sea / (1.0 + (damping / comps) * energy)
        energy = jnp.zeros_like(energy)
        if s + 1 == SRC_SUB:
            scale = scale * thaw
        for c in range(CHUNKS):
            at = pl.ds(c * chunk, chunk)
            growth = jnp.dot(matrix_ref[at, :], b_acc[s % 2], preferred_element_type=jnp.float32)
            value = (f_acc[at, :] + gain * growth) * scale
            f_acc[at, :] = value
            if s + 1 < SRC_SUB:
                b_acc[(s + 1) % 2, at, :] = value.astype(jnp.bfloat16)
                energy = energy + jnp.sum(value * value, axis=0, keepdims=True)
            elif ready is not None:
                ready(c, at)


def hold(odd, block, column, moved, f_acc, b_acc, iota, total):
    width = iota.shape[1]
    columns = slice(column * width, (column + 1) * width)
    for t in range(0, BLOCK // SUB, 2):
        pair = [reorder(lambda index: moved[column, tile_at(odd, block, index), :], INVERSE, t + k, iota) for k in range(2)]
        both = jnp.concatenate(pair, axis=0)
        at = pl.ds(block * BLOCK + t * SUB, 2 * SUB)
        f_acc[at, columns] = both
        b_acc[0, at, columns] = both.astype(jnp.bfloat16)
        total = total + pair[0] * pair[0] + pair[1] * pair[1]
    return total


def far_kernel(last, odd_ref, sea_ref, ice_ref, wind_ref, trig_ref, matrix_ref, cross_ref, inner_ref, local_ref,
               far_ref, near_ref, f_acc, b_acc, moved):
    count, _, width = local_ref.shape
    iota = sublanes(width)
    odd = odd_ref[0]
    seas = spread_all(sea_ref, count)
    rows = range(NEAR, count)

    def advance(block, sums):
        for q, coefficients in enumerate(block_coefficients(trig_ref, block)):
            at = quadrant_at(block, q)
            across = coefficients[2]
            if INWARD[q]:
                value = get(cross_ref, 0, half_at(block, q))
                for r in range(SUBSTEPS):
                    value = seas[r] * (across * value)
                for r in rows:
                    put(moved, r - NEAR, at, get(local_ref, r, at) + value if r == NEAR else get(local_ref, r, at))
            else:
                halo = [get(inner_ref, j, half_at(block, q)) for j in range(SUBSTEPS)]
                first, second, after_two = first_two(q, coefficients, flow(q, seas), halo)
                third = seas[count - 3] * (across * after_two)
                for r, value in enumerate([None] * (count - 3) + [third, second, first]):
                    value = get(local_ref, r, at) if value is None else get(local_ref, r, at) + value
                    if r < NEAR:
                        put(near_ref, r, half_at(block, q), value)
                    else:
                        put(moved, r - NEAR, at, value)
        return tuple(hold(odd, block, i, moved, f_acc, b_acc, iota, total) for i, total in enumerate(sums))

    zero = jnp.zeros((SUB, width), jnp.float32)
    sums = lax.fori_loop(0, BLOCKS, advance, (zero,) * len(rows))
    source_steps(odd, rows, sums, sea_ref, ice_ref, wind_ref, matrix_ref, f_acc, b_acc)
    if last:
        for i in range(len(rows)):
            far_ref[i] = f_acc[:, i * width:(i + 1) * width]
        return

    def finish(block, carry):
        put_in_order(odd, block, lambda r, at: f_acc[at, r * width:(r + 1) * width], far_ref, range(len(rows)), iota)
        return carry

    lax.fori_loop(0, BLOCKS, finish, 0)


def near_kernel(last, odd_ref, sea_ref, ice_ref, wind_ref, trig_ref, matrix_ref, cross_in, late_in, local_ref, part_ref, far_ref, *refs):
    if last:
        out_ref, f_acc, b_acc, moved, sem = refs
    else:
        out_ref, cross_ref, f_acc, b_acc, moved = refs
    count, _, width = local_ref.shape
    iota = sublanes(width)
    odd = odd_ref[0]
    seas = spread_all(sea_ref, count)
    if last:
        copies = [pltpu.make_async_copy(far_ref.at[i], out_ref.at[counted(odd, NEAR + i, count)], sem.at[NEAR * CHUNKS + i])
                  for i in range(count - NEAR)]
        for copy in copies:
            copy.start()

    def advance(block, sums):
        for q, coefficients in enumerate(block_coefficients(trig_ref, block)):
            at, half = quadrant_at(block, q), half_at(block, q)
            if INWARD[q]:
                halo = [get(cross_in, 0, half)] + [get(late_in, j, half) for j in range(SUBSTEPS - 1)]
                for r, value in enumerate(first_two(q, coefficients, seas, halo)[:NEAR]):
                    put(moved, r, at, get(local_ref, r, at) + value)
            else:
                for r in range(NEAR):
                    put(moved, r, at, get(part_ref, r, half))
        return tuple(hold(odd, block, i, moved, f_acc, b_acc, iota, total) for i, total in enumerate(sums))

    zero = jnp.zeros((SUB, width), jnp.float32)
    sums = lax.fori_loop(0, BLOCKS, advance, (zero,) * NEAR)
    if last:
        def ready(c, at):
            for r in range(NEAR):
                copy = pltpu.make_async_copy(f_acc.at[at, pl.ds(r * width, width)], out_ref.at[counted(odd, r, count), at, :],
                                             sem.at[NEAR * c + r])
                copy.start()
                copies.append(copy)

        source_steps(odd, range(NEAR), sums, sea_ref, ice_ref, wind_ref, matrix_ref, f_acc, b_acc, ready)
        for copy in copies:
            copy.wait()
        return
    source_steps(odd, range(NEAR), sums, sea_ref, ice_ref, wind_ref, matrix_ref, f_acc, b_acc)

    def finish(block, carry):
        put_in_order(odd, block, lambda r, at: f_acc[at, r * width:(r + 1) * width], out_ref, range(NEAR), iota)
        first_message(block, out_ref, cross_ref)
        return carry

    lax.fori_loop(0, BLOCKS, finish, 0)


def on_device(spectrum, sea_mask, ice_mask, wind, source_matrix):
    size = lax.axis_size("comp")
    comps, count, width = spectrum.shape
    assert comps == K and count >= SUBSTEPS and size % 2 == 0
    odd = (lax.axis_index("comp") % 2).astype(jnp.int32).reshape(1)
    f = jnp.transpose(spectrum, (1, 0, 2))
    trig = pattern()
    outer_pairs = [(i, i + 1) for i in range(1, size - 1, 2)]
    inner_pairs = [(i, i + 1) for i in range(0, size, 2)]

    def swap(value, pairs):
        return lax.ppermute(value, "comp", pairs + [(j, i) for i, j in pairs])

    vmem = pl.BlockSpec(memory_space=pltpu.VMEM)
    hbm = pl.BlockSpec(memory_space=pltpu.HBM)
    dma = pltpu.SemaphoreType.DMA

    def call(kernel, name, args, outs, scratch_rows=0, scratch=(), in_space=vmem, out_space=vmem, scalar=True, cost=0):
        scratch = list(scratch)
        if scratch_rows:
            scratch = [pltpu.VMEM((K, scratch_rows * width), jnp.float32),
                       pltpu.VMEM((2, K, scratch_rows * width), jnp.bfloat16),
                       pltpu.VMEM((scratch_rows, K, width), jnp.float32)] + scratch
        outs = [out if hasattr(out, "dtype") else jax.ShapeDtypeStruct(out, jnp.float32) for out in outs]
        return pl.pallas_call(
            kernel, out_shape=outs, name=name,
            in_specs=[pl.BlockSpec(memory_space=pltpu.SMEM)] * scalar + [in_space] * len(args),
            out_specs=[out_space] * len(outs), scratch_shapes=scratch,
            cost_estimate=pl.CostEstimate(flops=cost, bytes_accessed=0, transcendentals=0) if cost else None,
            compiler_params=pltpu.CompilerParams(vmem_limit_bytes=24 * 1024 * 1024),
        )(*((odd,) if scalar else ()), *args)

    def half(number):
        return (number, K // 2, width)

    whole = jax.ShapeDtypeStruct((count, K, width), jnp.float32)
    operands = [pltpu.with_memory_space_constraint(x, pltpu.HBM) for x in (f, sea_mask, trig)]
    f, sea, trig, cross = call(
        first_kernel, "first_edges", operands, [whole, sea_mask, trig, half(1)],
        scratch=[pltpu.VMEM(x.shape, x.dtype) for x in (f, sea_mask, trig)] + [dma((2,)), dma((BLOCKS,))], in_space=hbm)
    rows = (f,)
    masks = (sea, ice_mask, wind, trig, source_matrix)
    for step in range(STEPS):
        last = step == STEPS - 1
        cross = swap(cross, outer_pairs)
        late, inner = call(late_kernel, "late_edges", (sea, trig) + rows, [half(SUBSTEPS - 1), half(SUBSTEPS)], scalar=False)
        late = swap(late, outer_pairs)
        inner = swap(inner, inner_pairs)
        local, = call(local_kernel, "local_rows", (sea, trig) + rows, [whole], scalar=False, cost=30000000000)
        far, part = call(functools.partial(far_kernel, last), "far_rows", masks + (cross, inner, local),
                         [(count - NEAR, K, width), half(NEAR)], count - NEAR)
        outs = [whole] if last else [(NEAR, K, width), half(1)]
        result = call(functools.partial(near_kernel, last), "near_rows", masks + (cross, late, local, part, far), outs, NEAR,
                      scratch=[dma((NEAR * CHUNKS + count - NEAR,))] if last else (), out_space=hbm if last else vmem)
        if last:
            return jnp.transpose(result[0], (1, 0, 2))
        rows, cross = (result[0], far), result[1]


def solution(mesh):
    return jax.shard_map(
        on_device,
        mesh=mesh,
        in_specs=(
            P(None, ("grp", "comp"), None),
            P(("grp", "comp"), None),
            P(("grp", "comp"), None),
            P(("grp", "comp"), None),
            P(),
        ),
        out_specs=P(None, ("grp", "comp"), None),
        check_vma=False,
    )
```

```python
import functools

import jax
import jax.numpy as jnp
import numpy as np
from jax import lax
from jax.experimental import pallas as pl
from jax.experimental.pallas import tpu as pltpu
from jax.sharding import PartitionSpec as P

NDIR = 36
NFREQ = 32
K = 1152
STEPS = 2
SUBSTEPS = 3
SRC_SUB = 3

source_rate = 0.5
damping = 0.5

SUB = 8
QUADRANTS = 4
ARC = NDIR // QUADRANTS
ARC_ROWS = SUB * ARC
BLOCK = QUADRANTS * ARC_ROWS
BLOCKS = K // BLOCK
HALF = BLOCK // 2
CHUNKS = 4
EAST = (True, False, False, True)
INWARD = (True, True, False, False)
NEAR = SUBSTEPS - 1


def source_row(row):
    quadrant, rest = divmod(row, ARC_ROWS)
    frequency, direction = divmod(rest, ARC)
    return frequency * NDIR + quadrant * ARC + direction


ORDER = [source_row(row) for row in range(BLOCK)]
INVERSE = [ORDER.index(row) for row in range(BLOCK)]


def reorder(read, order, tile, iota):
    pieces = {}
    for to, row in enumerate(order[tile * SUB:(tile + 1) * SUB]):
        pieces.setdefault((row // SUB, (to - row) % SUB), []).append(to)
    out = None
    for (index, shift), rows in pieces.items():
        value = read(index)
        if shift:
            value = pltpu.roll(value, shift, 0)
        out = value if out is None else jnp.where((iota >= rows[0]) & (iota <= rows[-1]), value, out)
    return out


def pattern():
    row = np.arange(ARC_ROWS)
    theta = 2.0 * np.pi * (row % ARC + 0.5) / NDIR
    slower = 0.6 * 0.65 / (NFREQ - 1) * (row // ARC)
    table = np.stack([np.cos(theta), np.sin(theta), slower]).astype(np.float32)
    return jnp.asarray(np.ascontiguousarray(np.broadcast_to(table[:, :, None], (3, ARC_ROWS, 128))))


def sublanes(width):
    return lax.broadcasted_iota(jnp.int32, (SUB, width), 0)


def counted(odd, i, count):
    return odd * (count - 1) + (1 - 2 * odd) * i


def tile_at(odd, block, index):
    q, i = divmod(index, ARC)
    return pl.ds(pl.multiple_of(block * BLOCK + counted(odd, q, QUADRANTS) * ARC_ROWS + i * SUB, SUB), SUB)


def quadrant_at(block, q):
    return pl.ds(block * BLOCK + q * ARC_ROWS, ARC_ROWS)


def half_at(block, q):
    return pl.ds(block * HALF + (q if INWARD[q] else QUADRANTS - 1 - q) * ARC_ROWS, ARC_ROWS)


def block_coefficients(trig_ref, block):
    frequency = (block * SUB).astype(jnp.float32)
    fastest = 0.6 * (0.35 + (0.65 / (NFREQ - 1)) * ((NFREQ - 1) - frequency))
    cosine, sine, slower = (trig_ref[i].reshape(ARC, SUB, -1) for i in range(3))
    one, other = (fastest - slower) * cosine, (fastest - slower) * sine
    staying = 1.0 - one - other
    return [(staying, one, other) if q % 2 == 0 else (staying, other, one) for q in range(QUADRANTS)]


def get(ref, r, at):
    return ref[r, at, :].reshape(ARC, SUB, -1)


def put(ref, r, at, value):
    ref[r, at, :] = value.reshape(ARC_ROWS, -1)


def beside(q, value):
    last = value.ndim - 1
    return pltpu.roll(value, 1 if EAST[q] else value.shape[last] - 1, last)


def flow(q, rows):
    return list(rows) if INWARD[q] else list(rows)[::-1]


def substep(q, coefficients, rows, seas, whole):
    staying, along, across = coefficients
    out = []
    for i, row in enumerate(rows):
        if i == 0 and not whole:
            continue
        value = staying * row + along * beside(q, row)
        if i:
            value = value + across * rows[i - 1]
        out.append(seas[i] * value)
    return out


def edges(q, coefficients, rows, seas):
    found = [rows[-1]]
    rows, seas = rows[-SUBSTEPS:], seas[-SUBSTEPS:]
    for _ in range(SUBSTEPS - 1):
        rows = substep(q, coefficients, rows, seas, False)
        seas = seas[1:]
        found.append(rows[-1])
    return found


def from_first(q, coefficients, seas, halo):
    staying, along, across = coefficients
    first = seas[0] * (across * halo)
    beside_first = beside(q, first)
    second = seas[1] * (across * first)
    beside_second = beside(q, seas[1]) * (across * beside_first)
    third = seas[2] * (across * second)
    first = seas[0] * (staying * first + along * beside_first)
    second = seas[1] * (staying * second + along * beside_second + across * first)
    first = seas[0] * (staying * first + along * beside(q, first))
    return first, second, third


def from_later(q, coefficients, seas, halo):
    staying, along, across = coefficients
    first = seas[0] * (across * halo[0])
    second = seas[1] * (across * first)
    return seas[0] * (staying * first + along * beside(q, first) + across * halo[1]), second


def reader(row_refs):
    if len(row_refs) == 1:
        whole, = row_refs
        return whole.shape, lambda r, at: get(whole, r, at)
    near, far = row_refs
    shape = (NEAR + far.shape[0],) + tuple(far.shape[1:])
    return shape, lambda r, at: get(near, r, at) if r < NEAR else get(far, r - NEAR, at)


def spread_all(ref, count):
    return [jnp.broadcast_to(ref[r:r + 1, :].astype(jnp.float32), (SUB, ref.shape[1])) for r in range(count)]


def put_in_order(odd, block, read, out_ref, rows, iota):
    for r in rows:
        for t in range(BLOCK // SUB):
            tile = reorder(lambda index: read(r, pl.ds(block * BLOCK + index * SUB, SUB)), ORDER, t, iota)
            out_ref[r, tile_at(odd, block, t), :] = tile


def first_kernel(odd_ref, f_hbm, sea_hbm, trig_hbm, f_ref, sea_ref, trig_ref, cross_ref, sea_raw, trig_raw, sem, block_sem):
    count, _, width = f_ref.shape
    odd = odd_ref[0]

    def row_copy(block, r):
        at = pl.ds(pl.multiple_of(block * BLOCK, BLOCK), BLOCK)
        return pltpu.make_async_copy(f_hbm.at[counted(odd, r, count), at, :], f_ref.at[r, at, :], block_sem.at[r, block])

    small = [pltpu.make_async_copy(sea_hbm, sea_raw, sem.at[0]), pltpu.make_async_copy(trig_hbm, trig_raw, sem.at[1])]
    for r in range(count):
        for block in range(BLOCKS):
            row_copy(block, r).start()
    for copy in small:
        copy.start()
    iota = sublanes(width)

    def body(block, carry):
        row_copy(block, 0).wait()
        for t in range(BLOCK // SUB):
            q, i = divmod(t, ARC)
            read = lambda index: f_ref[0, pl.ds(block * BLOCK + index * SUB, SUB), :]
            if not INWARD[q]:
                at = pl.ds(half_at(block, q).start + i * SUB, SUB)
                there = (QUADRANTS - 1 - q) * ARC + i
                cross_ref[0, at, :] = jnp.where(odd == 1, reorder(read, ORDER, there, iota), reorder(read, ORDER, t, iota))
        return carry

    lax.fori_loop(0, BLOCKS, body, 0)
    for copy in small:
        copy.wait()
    for r in range(count):
        sea_ref[r:r + 1, :] = sea_raw[pl.ds(counted(odd, r, count), 1), :]
    for i in range(2):
        trig_ref[i] = trig_raw[counted(odd, i, 2)]
    trig_ref[2] = trig_raw[2]
    for r in range(1, count):
        for block in range(BLOCKS):
            row_copy(block, r).wait()


def late_kernel(first, odd_ref, sea_ref, trig_ref, *refs):
    if first:
        raw_ref, cross_ref, inner_ref, f_ref = refs
        (count, _, width), row = reader((f_ref,))
        iota = sublanes(width)
    else:
        cross_ref, inner_ref = refs[-2:]
        (count, _, _), row = reader(refs[:-2])
    seas = spread_all(sea_ref, count)

    def body(block, carry):
        if first:
            put_in_order(odd_ref[0], block, lambda r, at: raw_ref[r, at, :], f_ref, range(count), iota)
        for q, coefficients in enumerate(block_coefficients(trig_ref, block)):
            rows = flow(q, [row(r, quadrant_at(block, q)) for r in range(count)])
            found = edges(q, coefficients, rows, flow(q, seas))
            for j in range(SUBSTEPS):
                if INWARD[q]:
                    put(inner_ref, j, half_at(block, q), found[j])
                elif j:
                    put(cross_ref, j - 1, half_at(block, q), found[j])
        return carry

    lax.fori_loop(0, BLOCKS, body, 0)


def local_kernel(sea_ref, trig_ref, *refs):
    (count, _, _), row = reader(refs[:-1])
    local_ref = refs[-1]
    seas = spread_all(sea_ref, count)

    def body(block, carry):
        for q, coefficients in enumerate(block_coefficients(trig_ref, block)):
            at = quadrant_at(block, q)
            rows = flow(q, [row(r, at) for r in range(count)])
            for _ in range(SUBSTEPS):
                rows = substep(q, coefficients, rows, flow(q, seas), True)
            for r, value in enumerate(flow(q, rows)):
                put(local_ref, r, at, value)
        return carry

    lax.fori_loop(0, BLOCKS, body, 0)


def lanes(ref, rows):
    return jnp.concatenate([ref[pl.ds(r, 1), :].astype(jnp.float32) for r in rows], axis=1)


def source_steps(odd, rows, sums, sea_ref, ice_ref, wind_ref, matrix_ref, f_acc, b_acc, ready=None):
    comps, count = f_acc.shape[0], sea_ref.shape[0]
    there = [counted(odd, r, count) for r in rows]
    sea, gain, thaw = lanes(sea_ref, rows), source_rate * lanes(wind_ref, there), 1.0 - 0.5 * lanes(ice_ref, there)
    energy = jnp.concatenate([jnp.sum(s, axis=0, keepdims=True) for s in sums], axis=1)
    chunk = comps // CHUNKS
    for s in range(SRC_SUB):
        scale = sea / (1.0 + (damping / comps) * energy)
        energy = jnp.zeros_like(energy)
        if s + 1 == SRC_SUB:
            scale = scale * thaw
        for c in range(CHUNKS):
            at = pl.ds(c * chunk, chunk)
            growth = jnp.dot(matrix_ref[at, :], b_acc[s % 2], preferred_element_type=jnp.float32)
            value = (f_acc[at, :] + gain * growth) * scale
            f_acc[at, :] = value
            if s + 1 < SRC_SUB:
                b_acc[(s + 1) % 2, at, :] = value.astype(jnp.bfloat16)
                energy = energy + jnp.sum(value * value, axis=0, keepdims=True)
            elif ready is not None:
                ready(c, at)


def hold(odd, block, column, moved, f_acc, b_acc, iota, total):
    width = iota.shape[1]
    columns = slice(column * width, (column + 1) * width)
    for t in range(0, BLOCK // SUB, 2):
        pair = [reorder(lambda index: moved[column, tile_at(odd, block, index), :], INVERSE, t + k, iota) for k in range(2)]
        both = jnp.concatenate(pair, axis=0)
        at = pl.ds(block * BLOCK + t * SUB, 2 * SUB)
        f_acc[at, columns] = both
        b_acc[0, at, columns] = both.astype(jnp.bfloat16)
        total = total + pair[0] * pair[0] + pair[1] * pair[1]
    return total


def far_kernel(last, odd_ref, sea_ref, ice_ref, wind_ref, trig_ref, matrix_ref, cross_ref, inner_ref, local_ref,
               far_ref, near_ref, f_acc, b_acc, moved):
    count, _, width = local_ref.shape
    iota = sublanes(width)
    odd = odd_ref[0]
    seas = spread_all(sea_ref, count)
    rows = range(NEAR, count)

    def advance(block, sums):
        for q, coefficients in enumerate(block_coefficients(trig_ref, block)):
            at, half = quadrant_at(block, q), half_at(block, q)
            values = [get(local_ref, r, at) for r in range(count)]
            halo = cross_ref if INWARD[q] else inner_ref
            shares = [from_first(q, coefficients, flow(q, seas), get(halo, 0, half))]
            if not INWARD[q]:
                shares.append(from_later(q, coefficients, flow(q, seas), [get(halo, j, half) for j in range(1, SUBSTEPS)]))
            for share in shares:
                for i, value in enumerate(share):
                    r = i if INWARD[q] else count - 1 - i
                    values[r] = values[r] + value
            for r, value in enumerate(values):
                if r < NEAR:
                    put(near_ref, r, at, value)
                else:
                    put(moved, r - NEAR, at, value)
        return tuple(hold(odd, block, i, moved, f_acc, b_acc, iota, total) for i, total in enumerate(sums))

    zero = jnp.zeros((SUB, width), jnp.float32)
    sums = lax.fori_loop(0, BLOCKS, advance, (zero,) * len(rows))
    source_steps(odd, rows, sums, sea_ref, ice_ref, wind_ref, matrix_ref, f_acc, b_acc)
    if last:
        for i in range(len(rows)):
            far_ref[i] = f_acc[:, i * width:(i + 1) * width]
        return

    def finish(block, carry):
        put_in_order(odd, block, lambda r, at: f_acc[at, r * width:(r + 1) * width], far_ref, range(len(rows)), iota)
        return carry

    lax.fori_loop(0, BLOCKS, finish, 0)


def near_kernel(last, odd_ref, sea_ref, ice_ref, wind_ref, trig_ref, matrix_ref, late_ref, part_ref, far_ref, *refs):
    if last:
        out_ref, f_acc, b_acc, moved, sem = refs
    else:
        out_ref, cross_ref, f_acc, b_acc, moved = refs
    count, width = NEAR + far_ref.shape[0], far_ref.shape[2]
    iota = sublanes(width)
    odd = odd_ref[0]
    seas = spread_all(sea_ref, count)
    if last:
        copies = [pltpu.make_async_copy(far_ref.at[i], out_ref.at[counted(odd, NEAR + i, count)], sem.at[NEAR * CHUNKS + i])
                  for i in range(count - NEAR)]
        for copy in copies:
            copy.start()

    def advance(block, sums):
        for q, coefficients in enumerate(block_coefficients(trig_ref, block)):
            at = quadrant_at(block, q)
            values = [get(part_ref, r, at) for r in range(NEAR)]
            if INWARD[q]:
                halo = [get(late_ref, j, half_at(block, q)) for j in range(SUBSTEPS - 1)]
                values = [v + share for v, share in zip(values, from_later(q, coefficients, seas, halo))]
            for r, value in enumerate(values):
                put(moved, r, at, value)
        return tuple(hold(odd, block, i, moved, f_acc, b_acc, iota, total) for i, total in enumerate(sums))

    zero = jnp.zeros((SUB, width), jnp.float32)
    sums = lax.fori_loop(0, BLOCKS, advance, (zero,) * NEAR)
    if last:
        def ready(c, at):
            for r in range(NEAR):
                copy = pltpu.make_async_copy(f_acc.at[at, pl.ds(r * width, width)], out_ref.at[counted(odd, r, count), at, :],
                                             sem.at[NEAR * c + r])
                copy.start()
                copies.append(copy)

        source_steps(odd, range(NEAR), sums, sea_ref, ice_ref, wind_ref, matrix_ref, f_acc, b_acc, ready)
        for copy in copies:
            copy.wait()
        return
    source_steps(odd, range(NEAR), sums, sea_ref, ice_ref, wind_ref, matrix_ref, f_acc, b_acc)

    def finish(block, carry):
        put_in_order(odd, block, lambda r, at: f_acc[at, r * width:(r + 1) * width], out_ref, range(NEAR), iota)
        for q in range(QUADRANTS):
            if not INWARD[q]:
                cross_ref[0, half_at(block, q), :] = out_ref[0, quadrant_at(block, q), :]
        return carry

    lax.fori_loop(0, BLOCKS, finish, 0)


def on_device(spectrum, sea_mask, ice_mask, wind, source_matrix):
    size = lax.axis_size("comp")
    comps, count, width = spectrum.shape
    assert comps == K and count >= SUBSTEPS and size % 2 == 0
    odd = (lax.axis_index("comp") % 2).astype(jnp.int32).reshape(1)
    f = jnp.transpose(spectrum, (1, 0, 2))
    trig = pattern()
    outer_pairs = [(i, i + 1) for i in range(1, size - 1, 2)]
    inner_pairs = [(i, i + 1) for i in range(0, size, 2)]

    def swap(value, pairs):
        return lax.ppermute(value, "comp", pairs + [(j, i) for i, j in pairs])

    vmem = pl.BlockSpec(memory_space=pltpu.VMEM)
    hbm = pl.BlockSpec(memory_space=pltpu.HBM)
    dma = pltpu.SemaphoreType.DMA

    def call(kernel, name, args, outs, scratch_rows=0, scratch=(), in_space=vmem, out_space=vmem, scalar=True, cost=0):
        scratch = list(scratch)
        if scratch_rows:
            scratch = [pltpu.VMEM((K, scratch_rows * width), jnp.float32),
                       pltpu.VMEM((2, K, scratch_rows * width), jnp.bfloat16),
                       pltpu.VMEM((scratch_rows, K, width), jnp.float32)] + scratch
        outs = [out if hasattr(out, "dtype") else jax.ShapeDtypeStruct(out, jnp.float32) for out in outs]
        return pl.pallas_call(
            kernel, out_shape=outs, name=name,
            in_specs=[pl.BlockSpec(memory_space=pltpu.SMEM)] * scalar + [in_space] * len(args),
            out_specs=[out_space] * len(outs), scratch_shapes=scratch,
            cost_estimate=pl.CostEstimate(flops=cost, bytes_accessed=0, transcendentals=0) if cost else None,
            compiler_params=pltpu.CompilerParams(vmem_limit_bytes=24 * 1024 * 1024),
        )(*((odd,) if scalar else ()), *args)

    def half(number):
        return (number, K // 2, width)

    whole = jax.ShapeDtypeStruct((count, K, width), jnp.float32)
    operands = [pltpu.with_memory_space_constraint(x, pltpu.HBM) for x in (f, sea_mask, trig)]
    f, sea, trig, cross = call(
        first_kernel, "first_edge", operands, [whole, sea_mask, trig, half(1)],
        scratch=[pltpu.VMEM(x.shape, x.dtype) for x in (sea_mask, trig)] + [dma((2,)), dma((count, BLOCKS))], in_space=hbm)
    rows = (f,)
    masks = (sea, ice_mask, wind, trig, source_matrix)
    for step in range(STEPS):
        first, last = step == 0, step == STEPS - 1
        cross = swap(cross, outer_pairs)
        late, inner, *ordered = call(functools.partial(late_kernel, first), "late_edges", (sea, trig) + rows,
                                     [half(SUBSTEPS - 1), half(SUBSTEPS)] + [whole] * first)
        rows = tuple(ordered) or rows
        late = swap(late, outer_pairs)
        inner = swap(inner, inner_pairs)
        local, = call(local_kernel, "local_rows", (sea, trig) + rows, [whole], scalar=False, cost=30000000000)
        far, part = call(functools.partial(far_kernel, last), "far_rows", masks + (cross, inner, local),
                         [(count - NEAR, K, width), (NEAR, K, width)], count - NEAR)
        outs = [whole] if last else [(NEAR, K, width), half(1)]
        result = call(functools.partial(near_kernel, last), "near_rows", masks + (late, part, far), outs, NEAR,
                      scratch=[dma((NEAR * CHUNKS + count - NEAR,))] if last else (), out_space=hbm if last else vmem)
        if last:
            return jnp.transpose(result[0], (1, 0, 2))
        rows, cross = (result[0], far), result[1]


def solution(mesh):
    return jax.shard_map(
        on_device,
        mesh=mesh,
        in_specs=(
            P(None, ("grp", "comp"), None),
            P(("grp", "comp"), None),
            P(("grp", "comp"), None),
            P(("grp", "comp"), None),
            P(),
        ),
        out_specs=P(None, ("grp", "comp"), None),
        check_vma=False,
    )
```

```python
import functools

import jax
import jax.numpy as jnp
import numpy as np
from jax import lax
from jax.experimental import pallas as pl
from jax.experimental.pallas import tpu as pltpu
from jax.sharding import PartitionSpec as P

NDIR = 36
NFREQ = 32
K = 1152
STEPS = 2
SUBSTEPS = 3
SRC_SUB = 3

source_rate = 0.5
damping = 0.5

SUB = 8
QUADRANTS = 4
ARC = NDIR // QUADRANTS
ARC_ROWS = SUB * ARC
BLOCK = QUADRANTS * ARC_ROWS
BLOCKS = K // BLOCK
HALF = BLOCK // 2
CHUNKS = 4
EAST = (True, False, False, True)
INWARD = (True, True, False, False)
EARLY = 2
NEAR = SUBSTEPS - EARLY


def source_row(row):
    quadrant, rest = divmod(row, ARC_ROWS)
    frequency, direction = divmod(rest, ARC)
    return frequency * NDIR + quadrant * ARC + direction


ORDER = [source_row(row) for row in range(BLOCK)]
INVERSE = [ORDER.index(row) for row in range(BLOCK)]


def reorder(read, order, tile, iota):
    pieces = {}
    for to, row in enumerate(order[tile * SUB:(tile + 1) * SUB]):
        pieces.setdefault((row // SUB, (to - row) % SUB), []).append(to)
    out = None
    for (index, shift), rows in pieces.items():
        value = read(index)
        if shift:
            value = pltpu.roll(value, shift, 0)
        out = value if out is None else jnp.where((iota >= rows[0]) & (iota <= rows[-1]), value, out)
    return out


def pattern():
    row = np.arange(ARC_ROWS)
    theta = 2.0 * np.pi * (row % ARC + 0.5) / NDIR
    slower = 0.6 * 0.65 / (NFREQ - 1) * (row // ARC)
    table = np.stack([np.cos(theta), np.sin(theta), slower]).astype(np.float32)
    return jnp.asarray(np.ascontiguousarray(np.broadcast_to(table[:, :, None], (3, ARC_ROWS, 128))))


def sublanes(width):
    return lax.broadcasted_iota(jnp.int32, (SUB, width), 0)


def counted(odd, i, count):
    return odd * (count - 1) + (1 - 2 * odd) * i


def tile_at(odd, block, index):
    q, i = divmod(index, ARC)
    return pl.ds(pl.multiple_of(block * BLOCK + counted(odd, q, QUADRANTS) * ARC_ROWS + i * SUB, SUB), SUB)


def quadrant_at(block, q):
    return pl.ds(block * BLOCK + q * ARC_ROWS, ARC_ROWS)


def half_at(block, q):
    return pl.ds(block * HALF + (q if INWARD[q] else QUADRANTS - 1 - q) * ARC_ROWS, ARC_ROWS)


def block_coefficients(trig_ref, block):
    frequency = (block * SUB).astype(jnp.float32)
    fastest = 0.6 * (0.35 + (0.65 / (NFREQ - 1)) * ((NFREQ - 1) - frequency))
    cosine, sine, slower = (trig_ref[i].reshape(ARC, SUB, -1) for i in range(3))
    one, other = (fastest - slower) * cosine, (fastest - slower) * sine
    staying = 1.0 - one - other
    return [(staying, one, other) if q % 2 == 0 else (staying, other, one) for q in range(QUADRANTS)]


def get(ref, r, at):
    return ref[r, at, :].reshape(ARC, SUB, -1)


def put(ref, r, at, value):
    ref[r, at, :] = value.reshape(ARC_ROWS, -1)


def beside(q, value):
    last = value.ndim - 1
    return pltpu.roll(value, 1 if EAST[q] else value.shape[last] - 1, last)


def flow(q, rows):
    return list(rows) if INWARD[q] else list(rows)[::-1]


def substep(q, coefficients, rows, seas, whole):
    staying, along, across = coefficients
    out = []
    for i, row in enumerate(rows):
        if i == 0 and not whole:
            continue
        value = staying * row + along * beside(q, row)
        if i:
            value = value + across * rows[i - 1]
        out.append(seas[i] * value)
    return out


def edges(q, coefficients, rows, seas, number):
    found = [rows[-1]]
    rows, seas = rows[-number:], seas[-number:]
    for _ in range(number - 1):
        rows = substep(q, coefficients, rows, seas, False)
        seas = seas[1:]
        found.append(rows[-1])
    return found


def shares(q, coefficients, seas, halo):
    staying, along, across = coefficients
    rows = []
    for j in range(SUBSTEPS):
        near = [None if value is None else beside(q, value) if known is None else known for value, known in rows]
        new = []
        for i in range(j + 1):
            own = rows[i][0] if i < len(rows) else None
            upstream = rows[i - 1][0] if i else halo[j]
            value = known = None
            if own is not None:
                value = staying * own + along * near[i]
            if upstream is not None:
                value = across * upstream if value is None else value + across * upstream
                if i and own is None and j + 1 < SUBSTEPS:
                    known = beside(q, seas[i]) * (across * near[i - 1])
            new.append((None if value is None else seas[i] * value, known))
        rows = new
    return [value for value, _ in rows]


def with_shares(q, values, part):
    values = list(values)
    for i, value in enumerate(part):
        r = i if INWARD[q] else len(values) - 1 - i
        if value is not None and 0 <= r < len(values):
            values[r] = values[r] + value
    return values


def outward_messages(block, row, count, seas, trig_ref, refs, start=0):
    places = [(ref, j) for ref in refs for j in range(ref.shape[0])]
    for q, coefficients in enumerate(block_coefficients(trig_ref, block)):
        if not INWARD[q]:
            rows = flow(q, [row(r, quadrant_at(block, q)) for r in range(count)])
            found = edges(q, coefficients, rows, flow(q, seas), start + len(places))
            for (ref, j), value in zip(places, found[start:]):
                put(ref, j, half_at(block, q), value)


def reader(row_refs):
    if len(row_refs) == 1:
        whole, = row_refs
        return whole.shape, lambda r, at: get(whole, r, at)
    near, far = row_refs
    number = near.shape[0]
    shape = (number + far.shape[0],) + tuple(far.shape[1:])
    return shape, lambda r, at: get(near, r, at) if r < number else get(far, r - number, at)


def spread_all(ref, count):
    return [jnp.broadcast_to(ref[r:r + 1, :].astype(jnp.float32), (SUB, ref.shape[1])) for r in range(count)]


def put_in_order(odd, block, read, out_ref, rows, iota):
    for r in rows:
        for t in range(BLOCK // SUB):
            tile = reorder(lambda index: read(r, pl.ds(block * BLOCK + index * SUB, SUB)), ORDER, t, iota)
            out_ref[r, tile_at(odd, block, t), :] = tile


def first_kernel(odd_ref, f_hbm, sea_hbm, trig_hbm, f_ref, sea_ref, trig_ref, cross_ref, f_raw, sea_raw, trig_raw, sem, block_sem):
    count, _, width = f_ref.shape
    odd = odd_ref[0]

    def block_copy(block):
        at = pl.ds(pl.multiple_of(block * BLOCK, BLOCK), BLOCK)
        return pltpu.make_async_copy(f_hbm.at[:, at, :], f_raw.at[:, at, :], block_sem.at[block])

    small = [pltpu.make_async_copy(sea_hbm, sea_raw, sem.at[0]), pltpu.make_async_copy(trig_hbm, trig_raw, sem.at[1])]
    for copy in small:
        copy.start()
    for block in range(BLOCKS):
        block_copy(block).start()
    for copy in small:
        copy.wait()
    for r in range(count):
        sea_ref[r:r + 1, :] = sea_raw[pl.ds(counted(odd, r, count), 1), :]
    for i in range(2):
        trig_ref[i] = trig_raw[counted(odd, i, 2)]
    trig_ref[2] = trig_raw[2]
    iota = sublanes(width)
    seas = spread_all(sea_ref, count)

    def body(block, carry):
        block_copy(block).wait()
        put_in_order(odd, block, lambda r, at: f_raw[counted(odd, r, count), at, :], f_ref, range(count), iota)
        outward_messages(block, lambda r, at: get(f_ref, r, at), count, seas, trig_ref, [cross_ref])
        return carry

    lax.fori_loop(0, BLOCKS, body, 0)


def late_kernel(sea_ref, trig_ref, *refs):
    cross_ref, inner_ref = refs[-2:]
    (count, _, _), row = reader(refs[:-2])
    seas = spread_all(sea_ref, count)

    def body(block, carry):
        outward_messages(block, row, count, seas, trig_ref, [cross_ref], EARLY)
        for q, coefficients in enumerate(block_coefficients(trig_ref, block)):
            if INWARD[q]:
                rows = flow(q, [row(r, quadrant_at(block, q)) for r in range(count)])
                for j, value in enumerate(edges(q, coefficients, rows, flow(q, seas), SUBSTEPS)):
                    put(inner_ref, j, half_at(block, q), value)
        return carry

    lax.fori_loop(0, BLOCKS, body, 0)


def outward_kernel(sea_ref, trig_ref, inner_ref, local_ref, out_ref):
    count = local_ref.shape[0]
    seas = spread_all(sea_ref, count)

    def body(block, carry):
        for q, coefficients in enumerate(block_coefficients(trig_ref, block)):
            if not INWARD[q]:
                at, half = quadrant_at(block, q), half_at(block, q)
                halo = [get(inner_ref, j, half) for j in range(SUBSTEPS)]
                values = [get(local_ref, r, at) for r in range(count)]
                for r, value in enumerate(with_shares(q, values, shares(q, coefficients, flow(q, seas), halo))):
                    put(out_ref, r, half, value)
        return carry

    lax.fori_loop(0, BLOCKS, body, 0)


def local_kernel(sea_ref, trig_ref, *refs):
    (count, _, _), row = reader(refs[:-1])
    local_ref = refs[-1]
    seas = spread_all(sea_ref, count)

    def body(block, carry):
        for q, coefficients in enumerate(block_coefficients(trig_ref, block)):
            at = quadrant_at(block, q)
            rows = flow(q, [row(r, at) for r in range(count)])
            for _ in range(SUBSTEPS):
                rows = substep(q, coefficients, rows, flow(q, seas), True)
            for r, value in enumerate(flow(q, rows)):
                put(local_ref, r, at, value)
        return carry

    lax.fori_loop(0, BLOCKS, body, 0)


def lanes(ref, rows):
    return jnp.concatenate([ref[pl.ds(r, 1), :].astype(jnp.float32) for r in rows], axis=1)


def source_steps(odd, rows, sums, sea_ref, ice_ref, wind_ref, matrix_ref, f_acc, b_acc, ready=None):
    comps, count = f_acc.shape[0], sea_ref.shape[0]
    there = [counted(odd, r, count) for r in rows]
    sea, gain, thaw = lanes(sea_ref, rows), source_rate * lanes(wind_ref, there), 1.0 - 0.5 * lanes(ice_ref, there)
    energy = jnp.concatenate([jnp.sum(s, axis=0, keepdims=True) for s in sums], axis=1)
    chunk = comps // CHUNKS
    for s in range(SRC_SUB):
        scale = sea / (1.0 + (damping / comps) * energy)
        energy = jnp.zeros_like(energy)
        if s + 1 == SRC_SUB:
            scale = scale * thaw
        for c in range(CHUNKS):
            at = pl.ds(c * chunk, chunk)
            growth = jnp.dot(matrix_ref[at, :], b_acc[s % 2], preferred_element_type=jnp.float32)
            value = (f_acc[at, :] + gain * growth) * scale
            f_acc[at, :] = value
            if s + 1 < SRC_SUB:
                b_acc[(s + 1) % 2, at, :] = value.astype(jnp.bfloat16)
                energy = energy + jnp.sum(value * value, axis=0, keepdims=True)
            elif ready is not None:
                ready(c, at)


def hold(odd, block, column, moved, f_acc, b_acc, iota, total):
    width = iota.shape[1]
    columns = slice(column * width, (column + 1) * width)
    for t in range(0, BLOCK // SUB, 2):
        pair = [reorder(lambda index: moved[column, tile_at(odd, block, index), :], INVERSE, t + k, iota) for k in range(2)]
        both = jnp.concatenate(pair, axis=0)
        at = pl.ds(block * BLOCK + t * SUB, 2 * SUB)
        f_acc[at, columns] = both
        b_acc[0, at, columns] = both.astype(jnp.bfloat16)
        total = total + pair[0] * pair[0] + pair[1] * pair[1]
    return total


def far_kernel(last, odd_ref, sea_ref, ice_ref, wind_ref, trig_ref, matrix_ref, cross_ref, outward_ref, local_ref,
               far_ref, part_ref, f_acc, b_acc, moved):
    (count, _, width), near, early = local_ref.shape, part_ref.shape[0], cross_ref.shape[0]
    iota = sublanes(width)
    odd = odd_ref[0]
    seas = spread_all(sea_ref, count)
    rows = range(near, count)

    def advance(block, sums):
        for q, coefficients in enumerate(block_coefficients(trig_ref, block)):
            at, half = quadrant_at(block, q), half_at(block, q)
            if INWARD[q]:
                halo = [get(cross_ref, j, half) if j < early else None for j in range(SUBSTEPS)]
                values = [get(local_ref, r, at) for r in range(count)]
                values = with_shares(q, values, shares(q, coefficients, seas, halo))
            else:
                values = [get(outward_ref, r, half) for r in range(count)]
            for r, value in enumerate(values):
                if r < near:
                    put(part_ref, r, at, value)
                else:
                    put(moved, r - near, at, value)
        return tuple(hold(odd, block, i, moved, f_acc, b_acc, iota, total) for i, total in enumerate(sums))

    zero = jnp.zeros((SUB, width), jnp.float32)
    sums = lax.fori_loop(0, BLOCKS, advance, (zero,) * len(rows))
    source_steps(odd, rows, sums, sea_ref, ice_ref, wind_ref, matrix_ref, f_acc, b_acc)
    if last:
        for i in range(len(rows)):
            far_ref[i] = f_acc[:, i * width:(i + 1) * width]
        return

    def finish(block, carry):
        put_in_order(odd, block, lambda r, at: f_acc[at, r * width:(r + 1) * width], far_ref, range(len(rows)), iota)
        return carry

    lax.fori_loop(0, BLOCKS, finish, 0)


def near_kernel(last, odd_ref, sea_ref, ice_ref, wind_ref, trig_ref, matrix_ref, late_ref, part_ref, far_ref, *refs):
    if last:
        out_ref, f_acc, b_acc, moved, sem = refs
    else:
        out_ref, message_ref, f_acc, b_acc, moved = refs
    near, late, (_, _, width) = part_ref.shape[0], late_ref.shape[0], far_ref.shape
    count = near + far_ref.shape[0]
    iota = sublanes(width)
    odd = odd_ref[0]
    seas = spread_all(sea_ref, count)
    if last:
        copies = [pltpu.make_async_copy(far_ref.at[i], out_ref.at[counted(odd, near + i, count)], sem.at[near * CHUNKS + i])
                  for i in range(count - near)]
        for copy in copies:
            copy.start()

    def advance(block, sums):
        for q, coefficients in enumerate(block_coefficients(trig_ref, block)):
            at = quadrant_at(block, q)
            values = [get(part_ref, r, at) for r in range(near)]
            if INWARD[q]:
                halo = [None] * (SUBSTEPS - late) + [get(late_ref, j, half_at(block, q)) for j in range(late)]
                values = with_shares(q, values, shares(q, coefficients, seas, halo))
            for r, value in enumerate(values):
                put(moved, r, at, value)
        return tuple(hold(odd, block, i, moved, f_acc, b_acc, iota, total) for i, total in enumerate(sums))

    zero = jnp.zeros((SUB, width), jnp.float32)
    sums = lax.fori_loop(0, BLOCKS, advance, (zero,) * near)
    if last:
        def ready(c, at):
            for r in range(near):
                copy = pltpu.make_async_copy(f_acc.at[at, pl.ds(r * width, width)], out_ref.at[counted(odd, r, count), at, :],
                                             sem.at[near * c + r])
                copy.start()
                copies.append(copy)

        source_steps(odd, range(near), sums, sea_ref, ice_ref, wind_ref, matrix_ref, f_acc, b_acc, ready)
        for copy in copies:
            copy.wait()
        return
    source_steps(odd, range(near), sums, sea_ref, ice_ref, wind_ref, matrix_ref, f_acc, b_acc)

    _, row = reader((out_ref, far_ref))

    def finish(block, carry):
        put_in_order(odd, block, lambda r, at: f_acc[at, r * width:(r + 1) * width], out_ref, range(near), iota)
        outward_messages(block, row, count, seas, trig_ref, [message_ref])
        return carry

    lax.fori_loop(0, BLOCKS, finish, 0)


def on_device(spectrum, sea_mask, ice_mask, wind, source_matrix):
    size = lax.axis_size("comp")
    comps, count, width = spectrum.shape
    assert comps == K and count >= SUBSTEPS and size % 2 == 0
    odd = (lax.axis_index("comp") % 2).astype(jnp.int32).reshape(1)
    f = jnp.transpose(spectrum, (1, 0, 2))
    trig = pattern()
    outer_pairs = [(i, i + 1) for i in range(1, size - 1, 2)]
    inner_pairs = [(i, i + 1) for i in range(0, size, 2)]

    def swap(value, pairs):
        return lax.ppermute(value, "comp", pairs + [(j, i) for i, j in pairs])

    vmem = pl.BlockSpec(memory_space=pltpu.VMEM)
    hbm = pl.BlockSpec(memory_space=pltpu.HBM)
    dma = pltpu.SemaphoreType.DMA

    def call(kernel, name, args, outs, scratch_rows=0, scratch=(), in_space=vmem, out_space=vmem, scalar=True, cost=0):
        scratch = list(scratch)
        if scratch_rows:
            scratch = [pltpu.VMEM((K, scratch_rows * width), jnp.float32),
                       pltpu.VMEM((2, K, scratch_rows * width), jnp.bfloat16),
                       pltpu.VMEM((scratch_rows, K, width), jnp.float32)] + scratch
        outs = [out if hasattr(out, "dtype") else jax.ShapeDtypeStruct(out, jnp.float32) for out in outs]
        return pl.pallas_call(
            kernel, out_shape=outs, name=name,
            in_specs=[pl.BlockSpec(memory_space=pltpu.SMEM)] * scalar + [in_space] * len(args),
            out_specs=[out_space] * len(outs), scratch_shapes=scratch,
            cost_estimate=pl.CostEstimate(flops=cost, bytes_accessed=0, transcendentals=0) if cost else None,
            compiler_params=pltpu.CompilerParams(vmem_limit_bytes=24 * 1024 * 1024),
        )(*((odd,) if scalar else ()), *args)

    def half(number):
        return (number, K // 2, width)

    whole = jax.ShapeDtypeStruct((count, K, width), jnp.float32)
    operands = [pltpu.with_memory_space_constraint(x, pltpu.HBM) for x in (f, sea_mask, trig)]
    f, sea, trig, cross = call(
        first_kernel, "first_edges", operands, [whole, sea_mask, trig, half(EARLY)],
        scratch=[pltpu.VMEM(x.shape, x.dtype) for x in (f, sea_mask, trig)] + [dma((2,)), dma((BLOCKS,))], in_space=hbm)
    rows = (f,)
    masks = (sea, ice_mask, wind, trig, source_matrix)
    for step in range(STEPS):
        last = step == STEPS - 1
        cross = swap(cross, outer_pairs)
        late, inner = call(late_kernel, "late_edges", (sea, trig) + rows, [half(NEAR), half(SUBSTEPS)], scalar=False)
        late = swap(late, outer_pairs)
        inner = swap(inner, inner_pairs)
        local, = call(local_kernel, "local_rows", (sea, trig) + rows, [whole], scalar=False, cost=30000000000)
        outward, = call(outward_kernel, "outward_rows", (sea, trig, inner, local), [half(count)], scalar=False)
        far, part = call(functools.partial(far_kernel, last), "far_rows", masks + (cross, outward, local),
                         [(count - NEAR, K, width), (NEAR, K, width)], count - NEAR)
        outs = [whole] if last else [(NEAR, K, width), half(EARLY)]
        result = call(functools.partial(near_kernel, last), "near_rows", masks + (late, part, far), outs, NEAR,
                      scratch=[dma((NEAR * CHUNKS + count - NEAR,))] if last else (), out_space=hbm if last else vmem)
        if last:
            return jnp.transpose(result[0], (1, 0, 2))
        rows, cross = (result[0], far), result[1]


def solution(mesh):
    return jax.shard_map(
        on_device,
        mesh=mesh,
        in_specs=(
            P(None, ("grp", "comp"), None),
            P(("grp", "comp"), None),
            P(("grp", "comp"), None),
            P(("grp", "comp"), None),
            P(),
        ),
        out_specs=P(None, ("grp", "comp"), None),
        check_vma=False,
    )
```

```python
import functools

import jax
import jax.numpy as jnp
import numpy as np
from jax import lax
from jax.experimental import pallas as pl
from jax.experimental.pallas import tpu as pltpu
from jax.sharding import PartitionSpec as P

NDIR = 36
NFREQ = 32
K = 1152
STEPS = 2
SUBSTEPS = 3
SRC_SUB = 3

source_rate = 0.5
damping = 0.5

SUB = 8
QUADRANTS = 4
ARC = NDIR // QUADRANTS
ARC_ROWS = SUB * ARC
BLOCK = QUADRANTS * ARC_ROWS
BLOCKS = K // BLOCK
HALF = BLOCK // 2
CHUNKS = BLOCKS
EAST = (True, False, False, True)
INWARD = (True, True, False, False)
EARLY = 2
NEAR = SUBSTEPS - EARLY


def source_row(row):
    quadrant, rest = divmod(row, ARC_ROWS)
    frequency, direction = divmod(rest, ARC)
    return frequency * NDIR + quadrant * ARC + direction


ORDER = [source_row(row) for row in range(BLOCK)]
INVERSE = [ORDER.index(row) for row in range(BLOCK)]


def reorder(read, order, tile, iota):
    pieces = {}
    for to, row in enumerate(order[tile * SUB:(tile + 1) * SUB]):
        pieces.setdefault((row // SUB, (to - row) % SUB), []).append(to)
    out = None
    for (index, shift), rows in pieces.items():
        value = read(index)
        if shift:
            value = pltpu.roll(value, shift, 0)
        out = value if out is None else jnp.where((iota >= rows[0]) & (iota <= rows[-1]), value, out)
    return out


def pattern(width):
    row = lax.broadcasted_iota(jnp.int32, (ARC_ROWS, width), 0)
    angle = [2.0 * np.pi * (d + 0.5) / NDIR for d in range(ARC)]
    frequency = jnp.zeros((ARC_ROWS, width), jnp.int32)
    for f in range(1, SUB):
        frequency = jnp.where(row >= f * ARC, f, frequency)
    direction = row - ARC * frequency
    tables = []
    for values in (np.cos(angle), np.sin(angle)):
        table = jnp.full((ARC_ROWS, width), float(values[0]), jnp.float32)
        for d in range(1, ARC):
            table = jnp.where(direction == d, float(values[d]), table)
        tables.append(table)
    return tables + [(0.6 * 0.65 / (NFREQ - 1)) * frequency.astype(jnp.float32)]


def sublanes(width):
    return lax.broadcasted_iota(jnp.int32, (SUB, width), 0)


def counted(odd, i, count):
    return odd * (count - 1) + (1 - 2 * odd) * i


def tile_at(odd, block, index):
    q, i = divmod(index, ARC)
    return pl.ds(pl.multiple_of(block * BLOCK + counted(odd, q, QUADRANTS) * ARC_ROWS + i * SUB, SUB), SUB)


def quadrant_at(block, q):
    return pl.ds(block * BLOCK + q * ARC_ROWS, ARC_ROWS)


def half_at(block, q):
    return pl.ds(block * HALF + (q if INWARD[q] else QUADRANTS - 1 - q) * ARC_ROWS, ARC_ROWS)


def block_coefficients(trig_ref, block):
    frequency = jnp.float32(block * SUB)
    fastest = 0.6 * (0.35 + (0.65 / (NFREQ - 1)) * ((NFREQ - 1) - frequency))
    cosine, sine, slower = (trig_ref[i].reshape(ARC, SUB, -1) for i in range(3))
    one, other = (fastest - slower) * cosine, (fastest - slower) * sine
    staying = 1.0 - one - other
    return [(staying, one, other) if q % 2 == 0 else (staying, other, one) for q in range(QUADRANTS)]


def get(ref, r, at):
    return ref[r, at, :].reshape(ARC, SUB, -1)


def put(ref, r, at, value):
    ref[r, at, :] = value.reshape(ARC_ROWS, -1)


def beside(q, value):
    last = value.ndim - 1
    return pltpu.roll(value, 1 if EAST[q] else value.shape[last] - 1, last)


def flow(q, rows):
    return list(rows) if INWARD[q] else list(rows)[::-1]


def substep(q, coefficients, rows, seas, whole):
    staying, along, across = coefficients
    out = []
    for i, row in enumerate(rows):
        if i == 0 and not whole:
            continue
        value = staying * row + along * beside(q, row)
        if i:
            value = value + across * rows[i - 1]
        out.append(seas[i] * value)
    return out


def edges(q, coefficients, rows, seas, number):
    found = [rows[-1]]
    rows, seas = rows[-number:], seas[-number:]
    for _ in range(number - 1):
        rows = substep(q, coefficients, rows, seas, False)
        seas = seas[1:]
        found.append(rows[-1])
    return found


def shares(q, coefficients, seas, halo):
    staying, along, across = coefficients
    rows = []
    for j in range(SUBSTEPS):
        near = [None if value is None else beside(q, value) if known is None else known for value, known in rows]
        new = []
        for i in range(j + 1):
            own = rows[i][0] if i < len(rows) else None
            upstream = rows[i - 1][0] if i else halo[j]
            value = known = None
            if own is not None:
                value = staying * own + along * near[i]
            if upstream is not None:
                value = across * upstream if value is None else value + across * upstream
                if i and own is None and j + 1 < SUBSTEPS:
                    known = beside(q, seas[i]) * (across * near[i - 1])
            new.append((None if value is None else seas[i] * value, known))
        rows = new
    return [value for value, _ in rows]


def with_shares(q, values, part):
    values = list(values)
    for i, value in enumerate(part):
        r = i if INWARD[q] else len(values) - 1 - i
        if value is not None and 0 <= r < len(values):
            values[r] = values[r] + value
    return values


def outward_messages(block, row, count, seas, trig_ref, refs, start=0):
    places = [(ref, j) for ref in refs for j in range(ref.shape[0])]
    for q, coefficients in enumerate(block_coefficients(trig_ref, block)):
        if not INWARD[q]:
            rows = flow(q, [row(r, quadrant_at(block, q)) for r in range(count)])
            found = edges(q, coefficients, rows, flow(q, seas), start + len(places))
            for (ref, j), value in zip(places, found[start:]):
                put(ref, j, half_at(block, q), value)


def reader(row_refs):
    if len(row_refs) == 1:
        whole, = row_refs
        return whole.shape, lambda r, at: get(whole, r, at)
    near, far = row_refs
    number = near.shape[0]
    shape = (number + far.shape[0],) + tuple(far.shape[1:])
    return shape, lambda r, at: get(near, r, at) if r < number else get(far, r - number, at)


def spread_all(ref, count):
    return [jnp.broadcast_to(ref[r:r + 1, :].astype(jnp.float32), (SUB, ref.shape[1])) for r in range(count)]


def put_in_order(odd, block, read, out_ref, rows, iota):
    for r in rows:
        for t in range(BLOCK // SUB):
            tile = reorder(lambda index: read(r, pl.ds(block * BLOCK + index * SUB, SUB)), ORDER, t, iota)
            out_ref[r, tile_at(odd, block, t), :] = tile


def first_kernel(odd_ref, f_hbm, sea_hbm, f_ref, rest_ref, sea_ref, trig_ref, cross_ref, f_raw, sea_raw, sem, block_sem):
    count, _, width = f_hbm.shape
    odd = odd_ref[0]

    def block_copy(block):
        at = pl.ds(pl.multiple_of(block * BLOCK, BLOCK), BLOCK)
        return pltpu.make_async_copy(f_hbm.at[pl.ds(odd * (count - EARLY), EARLY), at, :], f_raw.at[:, at, :], block_sem.at[block])

    sea_copy = pltpu.make_async_copy(sea_hbm, sea_raw, sem.at[0])
    rest_copy = pltpu.make_async_copy(f_hbm.at[pl.ds((1 - odd) * EARLY, count - EARLY)], rest_ref, sem.at[1])
    sea_copy.start()
    for block in range(BLOCKS):
        block_copy(block).start()
    rest_copy.start()
    cosine, sine, slower = pattern(width)
    trig_ref[0] = jnp.where(odd == 1, sine, cosine)
    trig_ref[1] = jnp.where(odd == 1, cosine, sine)
    trig_ref[2] = slower
    sea_copy.wait()
    for r in range(count):
        sea_ref[r:r + 1, :] = sea_raw[pl.ds(counted(odd, r, count), 1), :]
    iota = sublanes(width)
    seas = spread_all(sea_ref, EARLY)

    def body(block, carry):
        block_copy(block).wait()
        put_in_order(odd, block, lambda r, at: f_raw[counted(odd, r, EARLY), at, :], f_ref, range(EARLY), iota)
        outward_messages(block, lambda r, at: get(f_ref, r, at), EARLY, seas, trig_ref, [cross_ref])
        return carry

    lax.fori_loop(0, BLOCKS, body, 0)
    rest_copy.wait()


def late_kernel(first, odd_ref, sea_ref, trig_ref, *refs):
    if first:
        early_ref, raw_ref, cross_ref, inner_ref, rest_ref = refs
        own = early_ref, rest_ref
        iota, left = sublanes(raw_ref.shape[2]), raw_ref.shape[0]
    else:
        *own, cross_ref, inner_ref = refs
    (count, _, _), row = reader(own)
    odd = odd_ref[0]
    seas = spread_all(sea_ref, count)

    def body(block, carry):
        if first:
            put_in_order(odd, block, lambda r, at: raw_ref[counted(odd, r, left), at, :], rest_ref, range(left), iota)
        outward_messages(block, row, count, seas, trig_ref, [cross_ref], EARLY)
        for q, coefficients in enumerate(block_coefficients(trig_ref, block)):
            if INWARD[q]:
                rows = flow(q, [row(r, quadrant_at(block, q)) for r in range(count)])
                for j, value in enumerate(edges(q, coefficients, rows, flow(q, seas), SUBSTEPS)):
                    put(inner_ref, j, half_at(block, q), value)
        return carry

    lax.fori_loop(0, BLOCKS, body, 0)


def outward_kernel(sea_ref, trig_ref, inner_ref, local_ref, out_ref):
    count = local_ref.shape[0]
    seas = spread_all(sea_ref, count)

    def body(block, carry):
        for q, coefficients in enumerate(block_coefficients(trig_ref, block)):
            if not INWARD[q]:
                at, half = quadrant_at(block, q), half_at(block, q)
                halo = [get(inner_ref, j, half) for j in range(SUBSTEPS)]
                values = [get(local_ref, r, at) for r in range(count)]
                for r, value in enumerate(with_shares(q, values, shares(q, coefficients, flow(q, seas), halo))):
                    put(out_ref, r, half, value)
        return carry

    lax.fori_loop(0, BLOCKS, body, 0)


def local_kernel(sea_ref, trig_ref, *refs):
    (count, _, _), row = reader(refs[:-1])
    local_ref = refs[-1]
    seas = spread_all(sea_ref, count)

    def body(block, carry):
        for q, coefficients in enumerate(block_coefficients(trig_ref, block)):
            at = quadrant_at(block, q)
            rows = flow(q, [row(r, at) for r in range(count)])
            for _ in range(SUBSTEPS):
                rows = substep(q, coefficients, rows, flow(q, seas), True)
            for r, value in enumerate(flow(q, rows)):
                put(local_ref, r, at, value)
        return carry

    lax.fori_loop(0, BLOCKS, body, 0)


def lanes(ref, rows):
    return jnp.concatenate([ref[pl.ds(r, 1), :].astype(jnp.float32) for r in rows], axis=1)


def source_steps(odd, rows, sums, sea_ref, ice_ref, wind_ref, matrix_ref, f_acc, b_acc, ready=None):
    comps, count = f_acc.shape[0], sea_ref.shape[0]
    there = [counted(odd, r, count) for r in rows]
    sea, gain, thaw = lanes(sea_ref, rows), source_rate * lanes(wind_ref, there), 1.0 - 0.5 * lanes(ice_ref, there)
    energy = jnp.concatenate([jnp.sum(s, axis=0, keepdims=True) for s in sums], axis=1)
    chunk = comps // CHUNKS
    for s in range(SRC_SUB):
        scale = sea / (1.0 + (damping / comps) * energy)
        energy = jnp.zeros_like(energy)
        if s + 1 == SRC_SUB:
            scale = scale * thaw
        for c in range(CHUNKS):
            at = pl.ds(c * chunk, chunk)
            growth = jnp.dot(matrix_ref[at, :], b_acc[s % 2], preferred_element_type=jnp.float32)
            value = (f_acc[at, :] + gain * growth) * scale
            f_acc[at, :] = value
            if s + 1 < SRC_SUB:
                b_acc[(s + 1) % 2, at, :] = value.astype(jnp.bfloat16)
                energy = energy + jnp.sum(value * value, axis=0, keepdims=True)
            elif ready is not None:
                ready(c, at)


def hold(odd, block, column, moved, f_acc, b_acc, iota, total):
    width = iota.shape[1]
    columns = slice(column * width, (column + 1) * width)
    for t in range(0, BLOCK // SUB, 2):
        pair = [reorder(lambda index: moved[column, tile_at(odd, block, index), :], INVERSE, t + k, iota) for k in range(2)]
        both = jnp.concatenate(pair, axis=0)
        at = pl.ds(block * BLOCK + t * SUB, 2 * SUB)
        f_acc[at, columns] = both
        b_acc[0, at, columns] = both.astype(jnp.bfloat16)
        total = total + pair[0] * pair[0] + pair[1] * pair[1]
    return total


def far_kernel(last, odd_ref, sea_ref, ice_ref, wind_ref, trig_ref, matrix_ref, cross_ref, outward_ref, local_ref,
               far_ref, part_ref, f_acc, b_acc, moved):
    (count, _, width), near, early = local_ref.shape, part_ref.shape[0], cross_ref.shape[0]
    iota = sublanes(width)
    odd = odd_ref[0]
    seas = spread_all(sea_ref, count)
    rows = range(near, count)

    def advance(block, sums):
        for q, coefficients in enumerate(block_coefficients(trig_ref, block)):
            at, half = quadrant_at(block, q), half_at(block, q)
            if INWARD[q]:
                halo = [get(cross_ref, j, half) if j < early else None for j in range(SUBSTEPS)]
                values = [get(local_ref, r, at) for r in range(count)]
                values = with_shares(q, values, shares(q, coefficients, seas, halo))
            else:
                values = [get(outward_ref, r, half) for r in range(count)]
            for r, value in enumerate(values):
                if r < near:
                    put(part_ref, r, at, value)
                else:
                    put(moved, r - near, at, value)
        return tuple(hold(odd, block, i, moved, f_acc, b_acc, iota, total) for i, total in enumerate(sums))

    zero = jnp.zeros((SUB, width), jnp.float32)
    sums = lax.fori_loop(0, BLOCKS, advance, (zero,) * len(rows))
    def ready(block, at):
        if last:
            for i in range(len(rows)):
                far_ref[i, at, :] = f_acc[at, i * width:(i + 1) * width]
        else:
            put_in_order(odd, block, lambda r, at: f_acc[at, r * width:(r + 1) * width], far_ref, range(len(rows)), iota)

    source_steps(odd, rows, sums, sea_ref, ice_ref, wind_ref, matrix_ref, f_acc, b_acc, ready)


def near_kernel(last, odd_ref, sea_ref, ice_ref, wind_ref, trig_ref, matrix_ref, late_ref, part_ref, far_ref, *refs):
    if last:
        out_ref, f_acc, b_acc, moved, sem = refs
    else:
        out_ref, message_ref, f_acc, b_acc, moved = refs
    near, late, (_, _, width) = part_ref.shape[0], late_ref.shape[0], far_ref.shape
    count = near + far_ref.shape[0]
    iota = sublanes(width)
    odd = odd_ref[0]
    seas = spread_all(sea_ref, count)
    if last:
        copies = [pltpu.make_async_copy(far_ref.at[i], out_ref.at[counted(odd, near + i, count)], sem.at[near * CHUNKS + i])
                  for i in range(count - near)]
        for copy in copies:
            copy.start()

    def advance(block, sums):
        for q, coefficients in enumerate(block_coefficients(trig_ref, block)):
            at = quadrant_at(block, q)
            values = [get(part_ref, r, at) for r in range(near)]
            if INWARD[q]:
                halo = [None] * (SUBSTEPS - late) + [get(late_ref, j, half_at(block, q)) for j in range(late)]
                values = with_shares(q, values, shares(q, coefficients, seas, halo))
            for r, value in enumerate(values):
                put(moved, r, at, value)
        return tuple(hold(odd, block, i, moved, f_acc, b_acc, iota, total) for i, total in enumerate(sums))

    zero = jnp.zeros((SUB, width), jnp.float32)
    sums = lax.fori_loop(0, BLOCKS, advance, (zero,) * near)
    if last:
        def ready(c, at):
            for r in range(near):
                copy = pltpu.make_async_copy(f_acc.at[at, pl.ds(r * width, width)], out_ref.at[counted(odd, r, count), at, :],
                                             sem.at[near * c + r])
                copy.start()
                copies.append(copy)

        source_steps(odd, range(near), sums, sea_ref, ice_ref, wind_ref, matrix_ref, f_acc, b_acc, ready)
        for copy in copies:
            copy.wait()
        return
    _, row = reader((out_ref, far_ref))

    def finish(block, at):
        put_in_order(odd, block, lambda r, at: f_acc[at, r * width:(r + 1) * width], out_ref, range(near), iota)
        outward_messages(block, row, count, seas, trig_ref, [message_ref])

    source_steps(odd, range(near), sums, sea_ref, ice_ref, wind_ref, matrix_ref, f_acc, b_acc, finish)


def on_device(spectrum, sea_mask, ice_mask, wind, source_matrix):
    size = lax.axis_size("comp")
    comps, count, width = spectrum.shape
    assert comps == K and count >= SUBSTEPS and size % 2 == 0
    odd = (lax.axis_index("comp") % 2).astype(jnp.int32).reshape(1)
    f = jnp.transpose(spectrum, (1, 0, 2))
    trig = jax.ShapeDtypeStruct((3, ARC_ROWS, width), jnp.float32)
    outer_pairs = [(i, i + 1) for i in range(1, size - 1, 2)]
    inner_pairs = [(i, i + 1) for i in range(0, size, 2)]

    def swap(value, pairs):
        return lax.ppermute(value, "comp", pairs + [(j, i) for i, j in pairs])

    vmem = pl.BlockSpec(memory_space=pltpu.VMEM)
    hbm = pl.BlockSpec(memory_space=pltpu.HBM)
    dma = pltpu.SemaphoreType.DMA

    def call(kernel, name, args, outs, scratch_rows=0, scratch=(), in_space=vmem, out_space=vmem, scalar=True, cost=0):
        scratch = list(scratch)
        if scratch_rows:
            scratch = [pltpu.VMEM((K, scratch_rows * width), jnp.float32),
                       pltpu.VMEM((2, K, scratch_rows * width), jnp.bfloat16),
                       pltpu.VMEM((scratch_rows, K, width), jnp.float32)] + scratch
        outs = [out if hasattr(out, "dtype") else jax.ShapeDtypeStruct(out, jnp.float32) for out in outs]
        return pl.pallas_call(
            kernel, out_shape=outs, name=name,
            in_specs=[pl.BlockSpec(memory_space=pltpu.SMEM)] * scalar + [in_space] * len(args),
            out_specs=[out_space] * len(outs), scratch_shapes=scratch,
            cost_estimate=pl.CostEstimate(flops=cost, bytes_accessed=0, transcendentals=0) if cost else None,
            compiler_params=pltpu.CompilerParams(vmem_limit_bytes=24 * 1024 * 1024),
        )(*((odd,) if scalar else ()), *args)

    def half(number):
        return (number, K // 2, width)

    whole = jax.ShapeDtypeStruct((count, K, width), jnp.float32)
    rest = (count - EARLY, K, width)
    operands = [pltpu.with_memory_space_constraint(x, pltpu.HBM) for x in (f, sea_mask)]
    f, raw, sea, trig, cross = call(
        first_kernel, "first_edges", operands, [(EARLY, K, width), rest, sea_mask, trig, half(EARLY)],
        scratch=[pltpu.VMEM((EARLY, K, width), jnp.float32), pltpu.VMEM(sea_mask.shape, sea_mask.dtype), dma((2,)), dma((BLOCKS,))],
        in_space=hbm)
    rows = (f, raw)
    masks = (sea, ice_mask, wind, trig, source_matrix)
    for step in range(STEPS):
        first, last = step == 0, step == STEPS - 1
        cross = swap(cross, outer_pairs)
        late, inner, *more = call(functools.partial(late_kernel, first), "late_edges", (sea, trig) + rows,
                                  [half(NEAR), half(SUBSTEPS)] + [rest] * first)
        rows = (f, *more) if first else rows
        late = swap(late, outer_pairs)
        inner = swap(inner, inner_pairs)
        local, = call(local_kernel, "local_rows", (sea, trig) + rows, [whole], scalar=False, cost=30000000000)
        outward, = call(outward_kernel, "outward_rows", (sea, trig, inner, local), [half(count)], scalar=False)
        far, part = call(functools.partial(far_kernel, last), "far_rows", masks + (cross, outward, local),
                         [(count - NEAR, K, width), (NEAR, K, width)], count - NEAR)
        outs = [whole] if last else [(NEAR, K, width), half(EARLY)]
        result = call(functools.partial(near_kernel, last), "near_rows", masks + (late, part, far), outs, NEAR,
                      scratch=[dma((NEAR * CHUNKS + count - NEAR,))] if last else (), out_space=hbm if last else vmem)
        if last:
            return jnp.transpose(result[0], (1, 0, 2))
        rows, cross = (result[0], far), result[1]


def solution(mesh):
    return jax.shard_map(
        on_device,
        mesh=mesh,
        in_specs=(
            P(None, ("grp", "comp"), None),
            P(("grp", "comp"), None),
            P(("grp", "comp"), None),
            P(("grp", "comp"), None),
            P(),
        ),
        out_specs=P(None, ("grp", "comp"), None),
        check_vma=False,
    )
```

```python
import functools

import jax
import jax.numpy as jnp
import numpy as np
from jax import lax
from jax.experimental import pallas as pl
from jax.experimental.pallas import tpu as pltpu
from jax.sharding import PartitionSpec as P

NDIR = 36
NFREQ = 32
K = 1152
STEPS = 2
SUBSTEPS = 3
SRC_SUB = 3

source_rate = 0.5
damping = 0.5

SUB = 8
QUADRANTS = 4
ARC = NDIR // QUADRANTS
ARC_ROWS = SUB * ARC
BLOCK = QUADRANTS * ARC_ROWS
BLOCKS = K // BLOCK
HALF = BLOCK // 2
CHUNKS = BLOCKS
EAST = (True, False, False, True)
INWARD = (True, True, False, False)
EARLY = 2
NEAR = SUBSTEPS - EARLY


def source_row(row):
    quadrant, rest = divmod(row, ARC_ROWS)
    frequency, direction = divmod(rest, ARC)
    return frequency * NDIR + quadrant * ARC + direction


ORDER = [source_row(row) for row in range(BLOCK)]
INVERSE = [ORDER.index(row) for row in range(BLOCK)]


def reorder(read, order, tile, iota):
    pieces = {}
    for to, row in enumerate(order[tile * SUB:(tile + 1) * SUB]):
        pieces.setdefault((row // SUB, (to - row) % SUB), []).append(to)
    out = None
    for (index, shift), rows in pieces.items():
        value = read(index)
        if shift:
            value = pltpu.roll(value, shift, 0)
        out = value if out is None else jnp.where((iota >= rows[0]) & (iota <= rows[-1]), value, out)
    return out


def pattern(width):
    row = lax.broadcasted_iota(jnp.int32, (ARC_ROWS, width), 0)
    angle = [2.0 * np.pi * (d + 0.5) / NDIR for d in range(ARC)]
    frequency = jnp.zeros((ARC_ROWS, width), jnp.int32)
    for f in range(1, SUB):
        frequency = jnp.where(row >= f * ARC, f, frequency)
    direction = row - ARC * frequency
    tables = []
    for values in (np.cos(angle), np.sin(angle)):
        table = jnp.full((ARC_ROWS, width), float(values[0]), jnp.float32)
        for d in range(1, ARC):
            table = jnp.where(direction == d, float(values[d]), table)
        tables.append(table)
    return tables + [(0.6 * 0.65 / (NFREQ - 1)) * frequency.astype(jnp.float32)]


def sublanes(width):
    return lax.broadcasted_iota(jnp.int32, (SUB, width), 0)


def counted(odd, i, count):
    return odd * (count - 1) + (1 - 2 * odd) * i


def tile_at(odd, block, index):
    q, i = divmod(index, ARC)
    return pl.ds(pl.multiple_of(block * BLOCK + counted(odd, q, QUADRANTS) * ARC_ROWS + i * SUB, SUB), SUB)


def quadrant_at(block, q):
    return pl.ds(block * BLOCK + q * ARC_ROWS, ARC_ROWS)


def half_at(block, q):
    return pl.ds(block * HALF + (q if INWARD[q] else QUADRANTS - 1 - q) * ARC_ROWS, ARC_ROWS)


def block_coefficients(trig_ref, block):
    frequency = jnp.float32(block * SUB)
    fastest = 0.6 * (0.35 + (0.65 / (NFREQ - 1)) * ((NFREQ - 1) - frequency))
    cosine, sine, slower = (trig_ref[i].reshape(ARC, SUB, -1) for i in range(3))
    one, other = (fastest - slower) * cosine, (fastest - slower) * sine
    staying = 1.0 - one - other
    return [(staying, one, other) if q % 2 == 0 else (staying, other, one) for q in range(QUADRANTS)]


def get(ref, r, at):
    return ref[r, at, :].reshape(ARC, SUB, -1)


def put(ref, r, at, value):
    ref[r, at, :] = value.reshape(ARC_ROWS, -1)


def beside(q, value):
    last = value.ndim - 1
    return pltpu.roll(value, 1 if EAST[q] else value.shape[last] - 1, last)


def flow(q, rows):
    return list(rows) if INWARD[q] else list(rows)[::-1]


def substep(q, coefficients, rows, seas, whole):
    staying, along, across = coefficients
    out = []
    for i, row in enumerate(rows):
        if i == 0 and not whole:
            continue
        value = staying * row + along * beside(q, row)
        if i:
            value = value + across * rows[i - 1]
        out.append(seas[i] * value)
    return out


def edges(q, coefficients, rows, seas, number):
    found = [rows[-1]]
    rows, seas = rows[-number:], seas[-number:]
    for _ in range(number - 1):
        rows = substep(q, coefficients, rows, seas, False)
        seas = seas[1:]
        found.append(rows[-1])
    return found


def shares(beside_of, coefficients, seas, halo):
    staying, along, across = coefficients
    rows = []
    for j in range(SUBSTEPS):
        near = [None if value is None else beside_of(value) if known is None else known for value, known in rows]
        new = []
        for i in range(j + 1):
            own = rows[i][0] if i < len(rows) else None
            upstream = rows[i - 1][0] if i else halo[j]
            value = known = None
            if own is not None:
                value = staying * own + along * near[i]
            if upstream is not None:
                value = across * upstream if value is None else value + across * upstream
                if i and own is None and j + 1 < SUBSTEPS:
                    known = beside_of(seas[i]) * (across * near[i - 1])
            new.append((None if value is None else seas[i] * value, known))
        rows = new
    return [value for value, _ in rows]


def inward_shares(trig_ref, block, seas, halo):
    pair = [q for q in range(QUADRANTS) if INWARD[q]]
    coefficients = block_coefficients(trig_ref, block)
    stacked = [jnp.stack([coefficients[q][i] for q in pair]) for i in range(3)]

    def beside_of(value):
        if value.ndim == 2:
            return jnp.stack([beside(q, value)[None] for q in pair])
        return jnp.stack([beside(q, value[i]) for i, q in enumerate(pair)])

    found = shares(beside_of, stacked, seas, [None if refs is None else jnp.stack([get(*refs, half_at(block, q)) for q in pair])
                                              for refs in halo])
    return {q: [None if value is None else value[i] for value in found] for i, q in enumerate(pair)}


def with_shares(q, values, part):
    values = list(values)
    for i, value in enumerate(part):
        r = i if INWARD[q] else len(values) - 1 - i
        if value is not None and 0 <= r < len(values):
            values[r] = values[r] + value
    return values


def outward_messages(block, row, count, seas, trig_ref, refs, start=0):
    places = [(ref, j) for ref in refs for j in range(ref.shape[0])]
    for q, coefficients in enumerate(block_coefficients(trig_ref, block)):
        if not INWARD[q]:
            rows = flow(q, [row(r, quadrant_at(block, q)) for r in range(count)])
            found = edges(q, coefficients, rows, flow(q, seas), start + len(places))
            for (ref, j), value in zip(places, found[start:]):
                put(ref, j, half_at(block, q), value)


def reader(row_refs):
    if len(row_refs) == 1:
        whole, = row_refs
        return whole.shape, lambda r, at: get(whole, r, at)
    near, far = row_refs
    number = near.shape[0]
    shape = (number + far.shape[0],) + tuple(far.shape[1:])
    return shape, lambda r, at: get(near, r, at) if r < number else get(far, r - number, at)


def spread_all(ref, count):
    return [jnp.broadcast_to(ref[r:r + 1, :].astype(jnp.float32), (SUB, ref.shape[1])) for r in range(count)]


def put_in_order(odd, block, read, out_ref, rows, iota):
    for r in rows:
        for t in range(BLOCK // SUB):
            tile = reorder(lambda index: read(r, pl.ds(block * BLOCK + index * SUB, SUB)), ORDER, t, iota)
            out_ref[r, tile_at(odd, block, t), :] = tile


def first_kernel(odd_ref, f_hbm, sea_hbm, f_ref, rest_ref, sea_ref, trig_ref, cross_ref, f_raw, sea_raw, sem, block_sem):
    count, _, width = f_hbm.shape
    odd = odd_ref[0]

    def block_copy(block):
        at = pl.ds(pl.multiple_of(block * BLOCK, BLOCK), BLOCK)
        return pltpu.make_async_copy(f_hbm.at[pl.ds(odd * (count - EARLY), EARLY), at, :], f_raw.at[:, at, :], block_sem.at[block])

    sea_copy = pltpu.make_async_copy(sea_hbm, sea_raw, sem.at[0])
    rest_copy = pltpu.make_async_copy(f_hbm.at[pl.ds((1 - odd) * EARLY, count - EARLY)], rest_ref, sem.at[1])
    sea_copy.start()
    for block in range(BLOCKS):
        block_copy(block).start()
    rest_copy.start()
    cosine, sine, slower = pattern(width)
    trig_ref[0] = jnp.where(odd == 1, sine, cosine)
    trig_ref[1] = jnp.where(odd == 1, cosine, sine)
    trig_ref[2] = slower
    sea_copy.wait()
    for r in range(count):
        sea_ref[r:r + 1, :] = sea_raw[pl.ds(counted(odd, r, count), 1), :]
    iota = sublanes(width)
    seas = spread_all(sea_ref, EARLY)

    def body(block, carry):
        block_copy(block).wait()
        put_in_order(odd, block, lambda r, at: f_raw[counted(odd, r, EARLY), at, :], f_ref, range(EARLY), iota)
        outward_messages(block, lambda r, at: get(f_ref, r, at), EARLY, seas, trig_ref, [cross_ref])
        return carry

    lax.fori_loop(0, BLOCKS, body, 0)
    rest_copy.wait()


def late_kernel(first, odd_ref, sea_ref, trig_ref, *refs):
    if first:
        early_ref, raw_ref, cross_ref, inner_ref, rest_ref = refs
        own = early_ref, rest_ref
        iota, left = sublanes(raw_ref.shape[2]), raw_ref.shape[0]
    else:
        *own, cross_ref, inner_ref = refs
    (count, _, _), row = reader(own)
    odd = odd_ref[0]
    seas = spread_all(sea_ref, count)

    def body(block, carry):
        if first:
            put_in_order(odd, block, lambda r, at: raw_ref[counted(odd, r, left), at, :], rest_ref, range(left), iota)
        outward_messages(block, row, count, seas, trig_ref, [cross_ref], EARLY)
        for q, coefficients in enumerate(block_coefficients(trig_ref, block)):
            if INWARD[q]:
                rows = flow(q, [row(r, quadrant_at(block, q)) for r in range(count)])
                for j, value in enumerate(edges(q, coefficients, rows, flow(q, seas), SUBSTEPS)):
                    put(inner_ref, j, half_at(block, q), value)
        return carry

    lax.fori_loop(0, BLOCKS, body, 0)


def outward_kernel(sea_ref, trig_ref, inner_ref, local_ref, out_ref):
    count = local_ref.shape[0]
    seas = spread_all(sea_ref, count)

    def body(block, carry):
        for q, coefficients in enumerate(block_coefficients(trig_ref, block)):
            if not INWARD[q]:
                at, half = quadrant_at(block, q), half_at(block, q)
                halo = [get(inner_ref, j, half) for j in range(SUBSTEPS)]
                values = [get(local_ref, r, at) for r in range(count)]
                for r, value in enumerate(with_shares(q, values, shares(functools.partial(beside, q), coefficients, flow(q, seas), halo))):
                    put(out_ref, r, half, value)
        return carry

    lax.fori_loop(0, BLOCKS, body, 0)


def local_kernel(sea_ref, trig_ref, *refs):
    (count, _, _), row = reader(refs[:-1])
    local_ref = refs[-1]
    seas = spread_all(sea_ref, count)

    def body(block, carry):
        for q, coefficients in enumerate(block_coefficients(trig_ref, block)):
            at = quadrant_at(block, q)
            rows = flow(q, [row(r, at) for r in range(count)])
            for _ in range(SUBSTEPS):
                rows = substep(q, coefficients, rows, flow(q, seas), True)
            for r, value in enumerate(flow(q, rows)):
                put(local_ref, r, at, value)
        return carry

    lax.fori_loop(0, BLOCKS, body, 0)


def lanes(ref, rows):
    return jnp.concatenate([ref[pl.ds(r, 1), :].astype(jnp.float32) for r in rows], axis=1)


def source_steps(odd, rows, sums, sea_ref, ice_ref, wind_ref, matrix_ref, f_acc, b_acc, ready=None):
    comps, count = f_acc.shape[0], sea_ref.shape[0]
    there = [counted(odd, r, count) for r in rows]
    sea, gain, thaw = lanes(sea_ref, rows), source_rate * lanes(wind_ref, there), 1.0 - 0.5 * lanes(ice_ref, there)
    energy = jnp.concatenate([jnp.sum(s, axis=0, keepdims=True) for s in sums], axis=1)
    chunk = comps // CHUNKS
    for s in range(SRC_SUB):
        scale = sea / (1.0 + (damping / comps) * energy)
        energy = jnp.zeros_like(energy)
        if s + 1 == SRC_SUB:
            scale = scale * thaw
        for c in range(CHUNKS):
            at = pl.ds(c * chunk, chunk)
            growth = jnp.dot(matrix_ref[at, :], b_acc[s % 2], preferred_element_type=jnp.float32)
            value = (f_acc[at, :] + gain * growth) * scale
            f_acc[at, :] = value
            if s + 1 < SRC_SUB:
                b_acc[(s + 1) % 2, at, :] = value.astype(jnp.bfloat16)
                energy = energy + jnp.sum(value * value, axis=0, keepdims=True)
            elif ready is not None:
                ready(c, at)


def hold(odd, block, column, moved, f_acc, b_acc, iota, total):
    width = iota.shape[1]
    columns = slice(column * width, (column + 1) * width)
    for t in range(0, BLOCK // SUB, 2):
        pair = [reorder(lambda index: moved[column, tile_at(odd, block, index), :], INVERSE, t + k, iota) for k in range(2)]
        both = jnp.concatenate(pair, axis=0)
        at = pl.ds(block * BLOCK + t * SUB, 2 * SUB)
        f_acc[at, columns] = both
        b_acc[0, at, columns] = both.astype(jnp.bfloat16)
        total = total + pair[0] * pair[0] + pair[1] * pair[1]
    return total


def far_kernel(last, odd_ref, sea_ref, ice_ref, wind_ref, trig_ref, matrix_ref, cross_ref, outward_ref, local_ref,
               far_ref, part_ref, f_acc, b_acc, moved):
    (count, _, width), near, early = local_ref.shape, part_ref.shape[0], cross_ref.shape[0]
    iota = sublanes(width)
    odd = odd_ref[0]
    seas = spread_all(sea_ref, count)
    rows = range(near, count)

    def advance(block, sums):
        halo = [(cross_ref, j) if j < early else None for j in range(SUBSTEPS)]
        inward = inward_shares(trig_ref, block, seas, halo)
        for q in range(QUADRANTS):
            at, half = quadrant_at(block, q), half_at(block, q)
            if INWARD[q]:
                values = with_shares(q, [get(local_ref, r, at) for r in range(count)], inward[q])
            else:
                values = [get(outward_ref, r, half) for r in range(count)]
            for r, value in enumerate(values):
                if r < near:
                    put(part_ref, r, at, value)
                else:
                    put(moved, r - near, at, value)
        return tuple(hold(odd, block, i, moved, f_acc, b_acc, iota, total) for i, total in enumerate(sums))

    zero = jnp.zeros((SUB, width), jnp.float32)
    sums = lax.fori_loop(0, BLOCKS, advance, (zero,) * len(rows), unroll=True)
    def ready(block, at):
        if last:
            for i in range(len(rows)):
                far_ref[i, at, :] = f_acc[at, i * width:(i + 1) * width]
        else:
            put_in_order(odd, block, lambda r, at: f_acc[at, r * width:(r + 1) * width], far_ref, range(len(rows)), iota)

    source_steps(odd, rows, sums, sea_ref, ice_ref, wind_ref, matrix_ref, f_acc, b_acc, ready)


def near_kernel(last, odd_ref, sea_ref, ice_ref, wind_ref, trig_ref, matrix_ref, late_ref, part_ref, far_ref, *refs):
    if last:
        out_ref, f_acc, b_acc, moved, sem = refs
    else:
        out_ref, message_ref, f_acc, b_acc, moved = refs
    near, late, (_, _, width) = part_ref.shape[0], late_ref.shape[0], far_ref.shape
    count = near + far_ref.shape[0]
    iota = sublanes(width)
    odd = odd_ref[0]
    seas = spread_all(sea_ref, count)
    if last:
        copies = [pltpu.make_async_copy(far_ref.at[i], out_ref.at[counted(odd, near + i, count)], sem.at[near * CHUNKS + i])
                  for i in range(count - near)]
        for copy in copies:
            copy.start()

    def advance(block, sums):
        halo = [None] * (SUBSTEPS - late) + [(late_ref, j) for j in range(late)]
        inward = inward_shares(trig_ref, block, seas, halo)
        for q in range(QUADRANTS):
            at = quadrant_at(block, q)
            values = [get(part_ref, r, at) for r in range(near)]
            if INWARD[q]:
                values = with_shares(q, values, inward[q])
            for r, value in enumerate(values):
                put(moved, r, at, value)
        return tuple(hold(odd, block, i, moved, f_acc, b_acc, iota, total) for i, total in enumerate(sums))

    zero = jnp.zeros((SUB, width), jnp.float32)
    sums = lax.fori_loop(0, BLOCKS, advance, (zero,) * near, unroll=True)
    if last:
        def ready(c, at):
            for r in range(near):
                copy = pltpu.make_async_copy(f_acc.at[at, pl.ds(r * width, width)], out_ref.at[counted(odd, r, count), at, :],
                                             sem.at[near * c + r])
                copy.start()
                copies.append(copy)

        source_steps(odd, range(near), sums, sea_ref, ice_ref, wind_ref, matrix_ref, f_acc, b_acc, ready)
        for copy in copies:
            copy.wait()
        return
    _, row = reader((out_ref, far_ref))

    def finish(block, at):
        put_in_order(odd, block, lambda r, at: f_acc[at, r * width:(r + 1) * width], out_ref, range(near), iota)
        outward_messages(block, row, count, seas, trig_ref, [message_ref])

    source_steps(odd, range(near), sums, sea_ref, ice_ref, wind_ref, matrix_ref, f_acc, b_acc, finish)


def on_device(spectrum, sea_mask, ice_mask, wind, source_matrix):
    size = lax.axis_size("comp")
    comps, count, width = spectrum.shape
    assert comps == K and count >= SUBSTEPS and size % 2 == 0
    odd = (lax.axis_index("comp") % 2).astype(jnp.int32).reshape(1)
    f = jnp.transpose(spectrum, (1, 0, 2))
    trig = jax.ShapeDtypeStruct((3, ARC_ROWS, width), jnp.float32)
    outer_pairs = [(i, i + 1) for i in range(1, size - 1, 2)]
    inner_pairs = [(i, i + 1) for i in range(0, size, 2)]

    def swap(value, pairs):
        return lax.ppermute(value, "comp", pairs + [(j, i) for i, j in pairs])

    vmem = pl.BlockSpec(memory_space=pltpu.VMEM)
    hbm = pl.BlockSpec(memory_space=pltpu.HBM)
    dma = pltpu.SemaphoreType.DMA

    def call(kernel, name, args, outs, scratch_rows=0, scratch=(), in_space=vmem, out_space=vmem, scalar=True, cost=0):
        scratch = list(scratch)
        if scratch_rows:
            scratch = [pltpu.VMEM((K, scratch_rows * width), jnp.float32),
                       pltpu.VMEM((2, K, scratch_rows * width), jnp.bfloat16),
                       pltpu.VMEM((scratch_rows, K, width), jnp.float32)] + scratch
        outs = [out if hasattr(out, "dtype") else jax.ShapeDtypeStruct(out, jnp.float32) for out in outs]
        return pl.pallas_call(
            kernel, out_shape=outs, name=name,
            in_specs=[pl.BlockSpec(memory_space=pltpu.SMEM)] * scalar + [in_space] * len(args),
            out_specs=[out_space] * len(outs), scratch_shapes=scratch,
            cost_estimate=pl.CostEstimate(flops=cost, bytes_accessed=0, transcendentals=0) if cost else None,
            compiler_params=pltpu.CompilerParams(vmem_limit_bytes=24 * 1024 * 1024),
        )(*((odd,) if scalar else ()), *args)

    def half(number):
        return (number, K // 2, width)

    whole = jax.ShapeDtypeStruct((count, K, width), jnp.float32)
    rest = (count - EARLY, K, width)
    operands = [pltpu.with_memory_space_constraint(x, pltpu.HBM) for x in (f, sea_mask)]
    f, raw, sea, trig, cross = call(
        first_kernel, "first_edges", operands, [(EARLY, K, width), rest, sea_mask, trig, half(EARLY)],
        scratch=[pltpu.VMEM((EARLY, K, width), jnp.float32), pltpu.VMEM(sea_mask.shape, sea_mask.dtype), dma((2,)), dma((BLOCKS,))],
        in_space=hbm)
    rows = (f, raw)
    masks = (sea, ice_mask, wind, trig, source_matrix)
    for step in range(STEPS):
        first, last = step == 0, step == STEPS - 1
        cross = swap(cross, outer_pairs)
        late, inner, *more = call(functools.partial(late_kernel, first), "late_edges", (sea, trig) + rows,
                                  [half(NEAR), half(SUBSTEPS)] + [rest] * first)
        rows = (f, *more) if first else rows
        late = swap(late, outer_pairs)
        inner = swap(inner, inner_pairs)
        local, = call(local_kernel, "local_rows", (sea, trig) + rows, [whole], scalar=False, cost=30000000000)
        outward, = call(outward_kernel, "outward_rows", (sea, trig, inner, local), [half(count)], scalar=False)
        far, part = call(functools.partial(far_kernel, last), "far_rows", masks + (cross, outward, local),
                         [(count - NEAR, K, width), (NEAR, K, width)], count - NEAR)
        outs = [whole] if last else [(NEAR, K, width), half(EARLY)]
        result = call(functools.partial(near_kernel, last), "near_rows", masks + (late, part, far), outs, NEAR,
                      scratch=[dma((NEAR * CHUNKS + count - NEAR,))] if last else (), out_space=hbm if last else vmem)
        if last:
            return jnp.transpose(result[0], (1, 0, 2))
        rows, cross = (result[0], far), result[1]


def solution(mesh):
    return jax.shard_map(
        on_device,
        mesh=mesh,
        in_specs=(
            P(None, ("grp", "comp"), None),
            P(("grp", "comp"), None),
            P(("grp", "comp"), None),
            P(("grp", "comp"), None),
            P(),
        ),
        out_specs=P(None, ("grp", "comp"), None),
        check_vma=False,
    )
```
